256 devices in a mesh: dp: 32 (over y_lo, z, core), fsdp: 8 (over x, y_hi).
Axes of the slice: x: 4, y: 4 (y_hi: 2, y_lo: 2; y = y_hi * 2 + y_lo), z: 8, core: 2. Of those that a mesh axis runs over, the one named last changes fastest.
Arguments:
- hidden_in: bfloat16 [32768, 4096], P(('dp', 'fsdp')), may hold values from -6 to 6
- lengths: int32 [32], P('dp'), may hold values from 1 to 1024, 24576 in all
- cartridge: bfloat16 [2, 512, 1024], P(None, None, 'fsdp'), may hold values from -96 to 96
- norm_gain: float32 [4096], replicated, may hold values from 0.1 to 1.9
- w_query: bfloat16 [4096, 4096], P('dp', 'fsdp'), may hold values from -0.09375 to 0.09375
- w_keyval: bfloat16 [4096, 2, 1024], P('dp', None, 'fsdp'), may hold values from -0.09375 to 0.09375
- cotangent: bfloat16 [32768, 4096], P('dp', 'fsdp'), may hold values from -6 to 6
Outputs:
- attn_heads: bfloat16 [32768, 4096], P('dp', 'fsdp')
- cart_grad: float32 [2, 512, 1024], P(None, None, 'fsdp')
The draws below stay inside these ranges and needn't reach their ends.
Inputs may be any that keep to these rules, and one draw needn't show every extreme that they name: `lengths`: positions at or past a conversation's length are padding.
All inputs are finite; a program needn't handle non-finite values. No bound on the sum of `lengths` on one device may be relied on, other than what follows from the above.
Results may differ from the reference program's by a relative error of at most 0.0095.
The reference program's roundings to bfloat16 on the way (of `normed`, `prob_b`, `grad` and `d_score_b`) count: a program that leaves them out, or rounds other values in their place, can miss the bound.
Values may be sent and summed in bfloat16 or wider, within the bound.
A program may use at most 64 MiB of HBM per device.

```python
import math
import jax
import jax.numpy as jnp
import numpy as np
from jax import lax

D = 4096
HD = 128
CART = 512
SEQ = 1024
KV_HEADS = 8
QH = 32
N_DP = 32


def draw_cartridge(key, part):
    key = jax.random.fold_in(key, 11)
    shape_full = (2, CART, KV_HEADS * HD)
    drawn = jnp.clip(jax.random.normal(key, shape_full, jnp.float32), -4.0, 4.0)
    return drawn.astype(jnp.bfloat16)


def level_of(stream_key, extent, pieces, least, high):
    loudness, own = 1.0, jax.random.fold_in(stream_key, 6)
    for position, blocks in pieces:
        heights = jnp.exp(jax.random.uniform(jax.random.fold_in(own, position), (blocks,), jnp.float32, least / len(pieces), high / len(pieces)))
        loudness = loudness * jnp.repeat(heights, extent[position] // blocks).reshape([-1 if axis == position else 1 for axis in range(len(extent))])
    return loudness


def length_profile(count, total, bound, lean):
    weights = [(1 << 20) // math.isqrt(rank ** lean) + 1 for rank in range(2, count + 1)]
    surplus, holding = total - bound - (count - 1), [1] * (count - 1)
    while surplus > 0:
        free = [i for i in range(count - 1) if holding[i] < bound]
        pool, remaining = sum([weights[i] for i in free]), surplus
        for i in free:
            extra = min(bound - holding[i], max(1, remaining * weights[i] // pool), surplus)
            holding[i] = holding[i] + extra
            surplus = surplus - extra
    return np.array([bound] + holding)


def uneven(stream_key, amount, total, most, skew):
    if amount == 2:
        one = jax.random.randint(stream_key, (), max(1, total - most), min(most, total - 1) + 1)
        return jnp.stack([one, total - one])
    sizes = jnp.asarray(length_profile(amount, total, most, skew), jnp.int32)
    pairs = (amount - 1) // 2
    source_of, receiver = sizes[1:1 + 2 * pairs:2], sizes[2:2 + 2 * pairs:2]
    margin = jnp.minimum(source_of - 1, most - receiver)
    passed = jax.random.randint(jax.random.fold_in(stream_key, 1), (pairs,), 0, 1 << 20) % (margin + 1)
    sizes = sizes.at[1:1 + 2 * pairs:2].set(source_of - passed).at[2:2 + 2 * pairs:2].set(receiver + passed)
    return sizes[jax.random.permutation(jax.random.fold_in(stream_key, 2), amount)]


def scatter_about(stream_key, extent, scale, bound, shards=(), kind=jnp.bfloat16):
    factor_of = level_of(stream_key, extent, shards, -0.22, 0.18) if shards else 1.0
    entries = jax.random.normal(stream_key, extent, jnp.float32) * scale * factor_of
    return jnp.minimum(jnp.maximum(entries, -bound), bound).astype(kind)


def setup_inputs(seed: int = 0) -> dict:
    key_list = jax.random.split(jax.random.key(seed), 8)
    return {
        "hidden_in": scatter_about(key_list[0], (N_DP * SEQ, D), 1.0, 6.0, ((0, 256),)),
        "lengths": uneven(key_list[1], N_DP, (3 * N_DP * SEQ) // 4, SEQ, 1).astype(jnp.int32),
        "cartridge": draw_cartridge(jax.random.fold_in(key_list[7], 71), 0),
        "norm_gain": jnp.clip(1.0 + 0.18 * jax.random.normal(key_list[3], (D,), jnp.float32), 0.1, 1.9),
        "w_query": scatter_about(key_list[4], (D, QH * HD), D ** -0.5, 0.09375, ((0, 32), (1, 8))),
        "w_keyval": scatter_about(key_list[5], (D, 2, KV_HEADS * HD), D ** -0.5, 0.09375, ((0, 32), (2, 8))),
        "cotangent": scatter_about(key_list[6], (N_DP * SEQ, QH * HD), 1.0, 6.0, ((0, 32), (1, 8))),
    }


epsilon = 1e-05
rope_base = 500000.0

def rounded(value):
    return lax.optimization_barrier(value.astype(jnp.bfloat16))

def normalize(hidden, norm_gain):
    floated = hidden.astype(jnp.float32)
    inverse = lax.rsqrt(lax.optimization_barrier(jnp.mean(floated * floated, axis=-1, keepdims=True)) + epsilon)
    return (floated * inverse * norm_gain).astype(jnp.bfloat16)

def rotate(matrix, positions, turn_sign, head_dim):
    row_count = matrix.shape[0]
    half_dim = head_dim // 2
    per_head = matrix.reshape(row_count, -1, head_dim)
    exponent = jnp.arange(half_dim).astype(jnp.float32) * (-2.0 / head_dim)
    frequency = jnp.power(jnp.float32(rope_base), exponent)
    angles = positions.astype(jnp.float32)[:, None] * frequency[None, :]
    cosine = jnp.cos(angles)[:, None, :]
    sine_part = turn_sign * jnp.sin(angles)[:, None, :]
    front_half = per_head[..., :half_dim]
    back_half = per_head[..., half_dim:]
    turned = jnp.concatenate([front_half * cosine - back_half * sine_part, back_half * cosine + front_half * sine_part], axis=-1)
    return turned.reshape(row_count, -1)

def head_attention(query_h, key_h, value_h, grad_h, length, cart_len):
    tokens = query_h.shape[0]
    key_count = key_h.shape[0]
    score_scale = HD ** (-0.5)
    query_f = query_h.astype(jnp.float32)
    key_f = key_h.astype(jnp.float32)
    value_f = value_h.astype(jnp.float32)
    grad_f = grad_h.astype(jnp.float32)
    scores = jnp.einsum('tgd,kd->gtk', query_f, key_f) * score_scale
    key_index = jnp.arange(key_count)[None, :]
    query_index = jnp.arange(tokens)[:, None]
    allowed = (key_index < cart_len) | (key_index - cart_len <= query_index) & (key_index - cart_len < length)
    scores = jnp.where(allowed, scores, -jnp.inf)
    row_max = lax.optimization_barrier(jnp.max(scores, axis=-1, keepdims=True))
    exponent = jnp.exp(scores - row_max)
    attn_prob = exponent / lax.optimization_barrier(jnp.sum(exponent, axis=-1, keepdims=True))
    prob_b = rounded(attn_prob).astype(jnp.float32)
    mixed = jnp.einsum('gtk,kd->tgd', prob_b, value_f).astype(jnp.bfloat16)
    d_prob = jnp.einsum('tgd,kd->gtk', grad_f, value_f)
    d_value = jnp.einsum('gtk,tgd->kd', prob_b[:, :, :cart_len], grad_f)
    d_score = attn_prob * (d_prob - lax.optimization_barrier(jnp.sum(attn_prob * d_prob, axis=-1, keepdims=True)))
    d_score_b = rounded(d_score).astype(jnp.float32)
    d_key = jnp.einsum('gtk,tgd->kd', d_score_b[:, :, :cart_len], query_f) * score_scale
    return (mixed, d_key, d_value)

def conversation(hidden, length, upstream, cartridge, norm_gain, w_query, w_keyval):
    tokens = hidden.shape[0]
    cart_len = cartridge.shape[1]
    model_dim = hidden.shape[1]
    kv_heads = KV_HEADS
    positions = cart_len + jnp.arange(tokens)
    normed = normalize(hidden, norm_gain)
    query = rounded(rotate(jnp.dot(normed, w_query, preferred_element_type=jnp.float32), positions, 1.0, HD))
    pair = jnp.dot(normed, w_keyval.reshape(model_dim, -1), preferred_element_type=jnp.float32)
    half_width = pair.shape[1] // 2
    key_new = rounded(rotate(pair[:, :half_width], positions, 1.0, HD))
    value_new = rounded(pair[:, half_width:])
    key_rows = jnp.concatenate([cartridge[0], key_new], axis=0)
    value_rows = jnp.concatenate([cartridge[1], value_new], axis=0)
    key_count = key_rows.shape[0]
    live_rows = (jnp.arange(tokens) < length)[:, None]
    grad = jnp.where(live_rows, upstream, jnp.zeros_like(upstream))
    query_split = query.reshape(tokens, kv_heads, -1, HD).transpose(1, 0, 2, 3)
    grad_split = grad.reshape(tokens, kv_heads, -1, HD).transpose(1, 0, 2, 3)
    key_split = key_rows.reshape(key_count, kv_heads, HD).transpose(1, 0, 2)
    value_split = value_rows.reshape(key_count, kv_heads, HD).transpose(1, 0, 2)

    def per_head(items):
        query_h, key_h, value_h, grad_h = items
        return head_attention(query_h, key_h, value_h, grad_h, length, cart_len)
    mixed, d_key, d_value = lax.map(per_head, (query_split, key_split, value_split, grad_split))
    mixed_rows = mixed.transpose(1, 0, 2, 3).reshape(tokens, -1)
    key_grad = d_key.transpose(1, 0, 2).reshape(cart_len, -1)
    value_grad = d_value.transpose(1, 0, 2).reshape(cart_len, -1)
    return (mixed_rows, jnp.stack([key_grad, value_grad]))

def reference(hidden_in, lengths, cartridge, norm_gain, w_query, w_keyval, cotangent):
    hidden_conv = hidden_in.reshape(N_DP, SEQ, D)
    upstream_conv = cotangent.reshape(N_DP, SEQ, -1)

    def per_conversation(running, inputs):
        hidden, length, upstream = inputs
        mixed_rows, cart_terms = conversation(hidden, length, upstream, cartridge, norm_gain, w_query, w_keyval)
        return (running + cart_terms, mixed_rows)
    initial = jnp.zeros(cartridge.shape, jnp.float32)
    summed, mixed_all = lax.scan(per_conversation, initial, (hidden_conv, lengths, upstream_conv))
    return (mixed_all.reshape(N_DP * SEQ, -1), summed)
```

```python
import functools
import math

import jax
import jax.numpy as jnp
from jax import lax
from jax.experimental import pallas as pl
from jax.experimental.pallas import tpu as pltpu
from jax.sharding import PartitionSpec as P

HD = 128
MESH = pl.DeviceIdType.MESH
EPS = 1e-05
ROPE_BASE = 500000.0
F32 = jnp.float32
BF16 = jnp.bfloat16
ROWS = 256


def normalize(hidden, norm_gain):
    floated = hidden.astype(F32)
    inverse = lax.rsqrt(jnp.mean(floated * floated, axis=-1, keepdims=True) + EPS)
    return (floated * inverse * norm_gain).astype(BF16)


def rotate(matrix, positions, head_dim):
    row_count = matrix.shape[0]
    half_dim = head_dim // 2
    per_head = matrix.reshape(row_count, -1, head_dim)
    exponent = jnp.arange(half_dim).astype(F32) * (-2.0 / head_dim)
    frequency = jnp.power(jnp.float32(ROPE_BASE), exponent)
    angles = positions.astype(F32)[:, None] * frequency[None, :]
    cosine = jnp.cos(angles)[:, None, :]
    sine = jnp.sin(angles)[:, None, :]
    front, back = per_head[..., :half_dim], per_head[..., half_dim:]
    turned = jnp.concatenate([front * cosine - back * sine, back * cosine + front * sine], axis=-1)
    return turned.reshape(row_count, -1)


def attention_kernel(len_ref, q_ref, kn_ref, vn_ref, cart_ref, g_ref, o_ref, grad_ref, kx, vt):
    length = len_ref[0]
    cart = cart_ref.shape[1]
    seq = kn_ref.shape[0]
    heads = q_ref.shape[1] // HD
    scale = HD ** -0.5
    factor = scale * math.log2(math.e)
    nt = (((1,), (1,)), ((), ()))

    live = lax.broadcasted_iota(jnp.int32, (seq, HD), 0) < length
    kx[:cart] = cart_ref[0]
    kx[cart:] = jnp.where(live, kn_ref[...], jnp.broadcast_to(cart_ref[0, 0:1, :], (seq, HD)))
    vt[:HD, :cart] = cart_ref[1].astype(F32).T.astype(BF16)
    vt[:HD, cart:] = jnp.where(live, vn_ref[...].astype(F32), 0.0).T.astype(BF16)
    extra = vt.shape[0] - HD
    spot = lax.broadcasted_iota(jnp.int32, (extra, cart + seq), 1)
    vt[HD:] = jnp.where(spot < cart + length, 1.0, 0.0).astype(BF16)
    grad_ref[...] = jnp.zeros_like(grad_ref)

    for block in range(seq // ROWS):
        before = cart + block * ROWS
        rows = pl.ds(block * ROWS, ROWS)

        @pl.loop(0, heads)
        def _(head):
            columns = pl.ds(pl.multiple_of(head * HD, HD), HD)
            q = q_ref[rows, columns]
            g = g_ref[rows, columns]
            row = block * ROWS + lax.broadcasted_iota(jnp.int32, (ROWS, HD), 0)
            g = jnp.where(row < length, g, jnp.zeros_like(g))
            s_far = lax.dot_general(kx[:before], q, nt, preferred_element_type=F32)
            s_near = lax.dot_general(kx[before:before + ROWS], q, nt, preferred_element_type=F32)
            key = lax.broadcasted_iota(jnp.int32, (ROWS, ROWS), 0)
            query = lax.broadcasted_iota(jnp.int32, (ROWS, ROWS), 1)
            s_near = jnp.where(key <= query, s_near, -jnp.inf)
            top = jnp.maximum(
                jnp.max(s_far, axis=0, keepdims=True), jnp.max(s_near, axis=0, keepdims=True)
            )
            e_far = jnp.exp2((s_far - top) * factor)
            e_near = jnp.exp2((s_near - top) * factor)
            out = jnp.dot(vt[:, :before], e_far.astype(BF16), preferred_element_type=F32)
            out += jnp.dot(vt[:, before:before + ROWS], e_near.astype(BF16), preferred_element_type=F32)
            inverse = 1.0 / out[HD:HD + 1]
            out = out[:HD] * inverse
            o_ref[rows, columns] = out.T.astype(BF16)
            delta = jnp.sum(out * g.astype(F32).T, axis=0, keepdims=True)
            d_prob = lax.dot_general(cart_ref[1], g, nt, preferred_element_type=F32)
            prob = e_far[:cart] * inverse
            d_score = prob * (d_prob - delta)
            grad_ref[1] += jnp.dot(prob.astype(BF16), g, preferred_element_type=F32)
            grad_ref[0] += jnp.dot(d_score.astype(BF16), q, preferred_element_type=F32)

    grad_ref[0] = grad_ref[0] * scale


def attention(length, q, k_new, v_new, cartridge, g):
    vmem = pl.BlockSpec(memory_space=pltpu.VMEM)
    cart, seq = cartridge.shape[1], q.shape[0]
    return pl.pallas_call(
        attention_kernel,
        name="attention",
        out_shape=(
            jax.ShapeDtypeStruct(q.shape, BF16),
            jax.ShapeDtypeStruct((2, cart, HD), F32),
        ),
        in_specs=[pl.BlockSpec(memory_space=pltpu.SMEM)] + [vmem] * 5,
        out_specs=(vmem, vmem),
        scratch_shapes=[
            pltpu.VMEM((cart + seq, HD), BF16),
            pltpu.VMEM((HD + 16, cart + seq), BF16),
        ],
        compiler_params=pltpu.CompilerParams(vmem_limit_bytes=40 << 20),
    )(length, q, k_new, v_new, cartridge, g)


def reduce_kernel(chips, part_ref, sum_ref, from_core, half, to_chips, from_chips, mine, gathered, other,
                  core_send, core_recv, rs_send, rs_recv, ag_send, ag_recv):
    dp, fsdp = lax.axis_index("dp"), lax.axis_index("fsdp")
    chip, core = dp // 2, dp % 2
    rows = part_ref.shape[0] // 2
    share = rows // chips
    sibling = (chip * 2 + (1 - core), fsdp)

    def peer(step):
        return lax.rem(chip + step, chips)

    barrier = pltpu.get_barrier_semaphore()
    pl.semaphore_signal(barrier, inc=1, device_id=sibling, device_id_type=MESH)
    for step in range(1, chips):
        pl.semaphore_signal(barrier, inc=1, device_id=(peer(step) * 2 + core, fsdp), device_id_type=MESH)
    pl.semaphore_wait(barrier, chips)

    def send(src, dst, send_sem, recv_sem, target):
        copy = pltpu.make_async_remote_copy(
            src_ref=src, dst_ref=dst, send_sem=send_sem, recv_sem=recv_sem,
            device_id=target, device_id_type=MESH,
        )
        copy.start()
        return copy

    theirs = pl.ds(pl.multiple_of((1 - core) * rows, rows), rows)
    ours = pl.ds(pl.multiple_of(core * rows, rows), rows)
    copy = send(part_ref.at[theirs], from_core, core_send.at[0], core_recv.at[0], sibling)
    copy.wait()
    half[...] = (part_ref[ours] + from_core[...]).reshape(half.shape)
    to_chips[...] = half[...].astype(BF16)
    copies = [
        send(to_chips.at[peer(step)], from_chips.at[step], rs_send.at[step], rs_recv.at[step],
             (peer(step) * 2 + core, fsdp))
        for step in range(1, chips)
    ]
    total = half[chip]
    for step, copy in zip(range(1, chips), copies):
        copy.wait()
        total += from_chips[step].astype(F32)
    mine[...] = total.astype(BF16)
    gathered[chip] = total.astype(BF16)
    copies = [
        send(mine, gathered.at[chip], ag_send.at[step], ag_recv.at[step], (peer(step) * 2 + core, fsdp))
        for step in range(1, chips)
    ]
    for copy in copies:
        copy.wait()
    copy = send(gathered, other, core_send.at[1], core_recv.at[1], sibling)
    sum_ref[ours] = gathered[...].astype(F32).reshape(rows, HD)
    copy.wait()
    sum_ref[theirs] = other[...].astype(F32).reshape(rows, HD)


def reduce_over_dp(part, n_dp):
    chips = n_dp // 2
    rows = part.shape[0]
    share = rows // 2 // chips
    vmem = pl.BlockSpec(memory_space=pltpu.VMEM)
    dma = pltpu.SemaphoreType.DMA
    return pl.pallas_call(
        functools.partial(reduce_kernel, chips),
        name="reduce_over_dp",
        out_shape=jax.ShapeDtypeStruct(part.shape, F32),
        in_specs=[vmem],
        out_specs=vmem,
        scratch_shapes=[
            pltpu.VMEM((rows // 2, HD), F32),
            pltpu.VMEM((chips, share, HD), F32),
            pltpu.VMEM((chips, share, HD), BF16),
            pltpu.VMEM((chips, share, HD), BF16),
            pltpu.VMEM((share, HD), BF16),
            pltpu.VMEM((chips, share, HD), BF16),
            pltpu.VMEM((chips, share, HD), BF16),
            dma((2,)), dma((2,)), dma((chips,)), dma((chips,)), dma((chips,)), dma((chips,)),
        ],
        compiler_params=pltpu.CompilerParams(collective_id=1, has_side_effects=True),
    )(part)


def on_device(n_dp, hidden_in, lengths, cartridge, norm_gain, w_query, w_keyval, cotangent):
    cart = cartridge.shape[1]
    normed = normalize(hidden_in, norm_gain)
    query_weight = lax.all_gather(w_query, "dp", axis=0, tiled=True)
    pair_weight = lax.all_gather(w_keyval, "dp", axis=0, tiled=True)
    piece = lax.all_gather(normed, "fsdp", axis=0, tiled=True)
    spots = cart + jnp.arange(piece.shape[0])
    query_sum = jnp.dot(piece, query_weight, preferred_element_type=F32)
    pair_sum = jnp.dot(piece, pair_weight.reshape(pair_weight.shape[0], -1), preferred_element_type=F32)
    query = rotate(query_sum, spots, HD).astype(BF16)
    key_new = rotate(pair_sum[:, :HD], spots, HD).astype(BF16)
    value_new = pair_sum[:, HD:].astype(BF16)
    mixed, part = attention(lengths, query, key_new, value_new, cartridge, cotangent)
    summed = reduce_over_dp(part.reshape(-1, HD), n_dp)
    return mixed, summed.reshape(2, cart, HD)


def solution(mesh):
    in_specs = (
        P(("dp", "fsdp"), None),
        P("dp"),
        P(None, None, "fsdp"),
        P(),
        P("dp", "fsdp"),
        P("dp", None, "fsdp"),
        P("dp", "fsdp"),
    )
    out_specs = (P("dp", "fsdp"), P(None, None, "fsdp"))
    return jax.shard_map(
        functools.partial(on_device, mesh.shape["dp"]),
        mesh=mesh, in_specs=in_specs, out_specs=out_specs, check_vma=False,
    )
```

```python
import functools
import math

import jax
import jax.numpy as jnp
import numpy as np
from jax import lax
from jax.experimental import pallas as pl
from jax.experimental.pallas import tpu as pltpu
from jax.sharding import PartitionSpec as P

HD = 128
MESH = pl.DeviceIdType.MESH
EPS = 1e-05
ROPE_BASE = 500000.0
F32 = jnp.float32
BF16 = jnp.bfloat16
ROWS = 256


def project_kernel(hidden_ref, gain_ref, wq_ref, wkv_ref, cos_ref, sin_ref, q_ref, k_ref, v_ref,
                   xn, wq, wkv, acc_q, acc_kv, q_out, kv_out, q_in, kv_in, local_sem, send_sem, recv_sem):
    dp, fsdp = lax.axis_index("dp"), lax.axis_index("fsdp")
    x, y_hi, y_lo, z, c = fsdp // 2, fsdp % 2, dp // 16, (dp // 2) % 8, dp % 2
    y = y_hi * 2 + y_lo
    turn = 1 - 2 * c

    def at(dx=0, dy=0, dz=0, other=False):
        yy = lax.rem(y + dy + 8, 4)
        return (
            lax.rem(yy, 2) * 16 + lax.rem(z + dz + 16, 8) * 2 + (1 - c if other else c),
            lax.rem(x + dx + 8, 4) * 2 + yy // 2,
        )

    def zs(r):
        return lax.rem(z + r + 16, 8)

    def ys(dy):
        yy = lax.rem(y + dy + 8, 4)
        return yy // 2, lax.rem(yy, 2)

    def xs(dx):
        return lax.rem(x + dx + 8, 4)

    slots, started = {}, []

    def send(name, ref, target, dst=None):
        assert name not in slots
        copy = pltpu.make_async_remote_copy(
            src_ref=ref, dst_ref=ref if dst is None else dst,
            send_sem=send_sem.at[len(started)], recv_sem=recv_sem.at[len(started)],
            device_id=target, device_id_type=MESH,
        )
        copy.start()
        slots[name] = copy
        started.append(copy)

    def arrived(name):
        slots[name].wait_recv()

    def wq_at(dy, r, core=None):
        hi, lo = ys(dy)
        return wq.at[hi, lo, zs(r), c if core is None else core]

    def wkv_at(dy, r):
        hi, lo = ys(dy)
        return wkv.at[hi, lo, zs(r), c]

    own_q = pltpu.make_async_copy(wq_ref, wq_at(0, 0), local_sem.at[0])
    own_kv = pltpu.make_async_copy(wkv_ref, wkv_at(0, 0), local_sem.at[1])
    own_q.start()
    own_kv.start()
    barrier = pltpu.get_barrier_semaphore()
    partners = [at(dx=1), at(dx=-1), at(dy=1), at(dy=-1), at(dy=2), at(dz=1), at(dz=-1), at(other=True)]
    for partner in partners:
        pl.semaphore_signal(barrier, inc=1, device_id=partner, device_id_type=MESH)
    pl.semaphore_wait(barrier, len(partners))
    own_q.wait()
    own_kv.wait()

    def ticks(i):
        return {0: [0], 4: [4]}.get(i, [i, -i])

    def wq_from_z(i):
        if i == 4:
            arrived(("zq", 4, 0))
            arrived(("zq", 4, 1))
        elif i:
            arrived(("zq", i))
            arrived(("zq", -i))
        if i < 3:
            send(("zq", i + 1), wq_at(0, i), at(dz=-1))
            send(("zq", -i - 1), wq_at(0, -i), at(dz=1))
        elif i == 3:
            send(("zq", 4, 0), wq_at(0, 3).at[pl.ds(0, 64)], at(dz=-1))
            send(("zq", 4, 1), wq_at(0, -3).at[pl.ds(64, 64)], at(dz=1))
        for r in ticks(i):
            send(("yq", -1, r), wq_at(0, r), at(dy=1))
            send(("yq", 1, r), wq_at(0, r), at(dy=-1))

    def wq_from_y(i):
        for r in ticks(i):
            arrived(("yq", -1, r))
            arrived(("yq", 1, r))
            way = turn if r in (0, 4) else (1 if r > 0 else -1)
            send(("yq", 2, r), wq_at(way, r), at(dy=-way))

    def wq_to_core(i):
        for r in ticks(i):
            arrived(("yq", 2, r))
            send(("cq", r), wq.at[:, :, zs(r), c], at(other=True))

    def wkv_from_z(i):
        if i == 4:
            arrived(("zk", 4, 0))
            arrived(("zk", 4, 1))
        elif i:
            arrived(("zk", i))
            arrived(("zk", -i))
        if i < 3:
            send(("zk", i + 1), wkv.at[:, :, zs(i), c], at(dz=-1))
            send(("zk", -i - 1), wkv.at[:, :, zs(-i), c], at(dz=1))
        elif i == 3:
            send(("zk", 4, 0), wkv.at[0, :, zs(3), c], at(dz=-1))
            send(("zk", 4, 1), wkv.at[1, :, zs(-3), c], at(dz=1))
        for r in ticks(i):
            send(("ck", r), wkv.at[:, :, zs(r), c], at(other=True))

    def rows_out(i):
        for r in ticks(i):
            send(("x", -1, r), xn.at[:, zs(r), x], at(dx=1))
            send(("x", 1, r), xn.at[:, zs(r), x], at(dx=-1))

    def rows_on(i):
        for r in ticks(i):
            arrived(("x", -1, r))
            arrived(("x", 1, r))
            send(("x", 2, r, 0), xn.at[0, zs(r), xs(1)], at(dx=-1))
            send(("x", 2, r, 1), xn.at[1, zs(r), xs(-1)], at(dx=1))

    def multiply(i, halves=(0, 1)):
        for r in ticks(i):
            arrived(("cq", r))
            arrived(("ck", r))
            arrived(("x", 2, r, 0))
            arrived(("x", 2, r, 1))
        for r in ticks(i):
            spot = zs(r)
            left = jnp.concatenate([xn[lo, spot].reshape(512, 256) for lo in range(2)], axis=1)
            for hi in range(2):
                right = jnp.concatenate([wq[hi, lo, spot].reshape(256, 512) for lo in range(2)], axis=0)
                term = jnp.dot(left, right, preferred_element_type=F32)
                acc_q[hi] = term if r == 0 else acc_q[hi] + term
                right = jnp.concatenate([wkv[hi, lo, spot].reshape(256, 256) for lo in range(2)], axis=0)
                term = jnp.dot(left, right, preferred_element_type=F32)
                acc_kv[hi] = term if r == 0 else acc_kv[hi] + term

    wq_from_z(0)
    send(("yk", -1), wkv_at(0, 0), at(dy=1))
    send(("yk", 1), wkv_at(0, 0), at(dy=-1))
    hidden = hidden_ref[...].astype(F32)
    inverse = lax.rsqrt(jnp.mean(hidden * hidden, axis=-1, keepdims=True) + EPS)
    for k in range(16):
        cols = slice(k * 256, (k + 1) * 256)
        part = hidden_ref[:, cols].astype(F32) * inverse * gain_ref[:, cols]
        xn[k // 8, k % 8, x] = part.astype(BF16)
    rows_out(0)
    rows_out(1)
    arrived(("yk", -1))
    arrived(("yk", 1))
    send(("yk", 2), wkv_at(turn, 0), at(dy=-turn))
    wq_from_z(1)
    wq_from_y(0)
    rows_on(0)
    rows_out(2)
    arrived(("yk", 2))
    wkv_from_z(0)
    wq_to_core(0)
    wq_from_z(2)
    wq_from_y(1)
    rows_on(1)
    rows_out(3)
    multiply(0)
    wkv_from_z(1)
    wq_from_z(3)
    wq_to_core(1)
    wq_from_y(2)
    rows_on(2)
    rows_out(4)
    multiply(1)
    wkv_from_z(2)
    wq_from_z(4)
    wq_to_core(2)
    wq_from_y(3)
    rows_on(3)
    multiply(2)
    wkv_from_z(3)
    wq_to_core(3)
    wq_from_y(4)
    rows_on(4)
    multiply(3)
    wkv_from_z(4)
    wq_to_core(4)
    multiply(4)

    cos = cos_ref[:, y_hi].reshape(512, HD)
    sin = sin_ref[:, y_hi].reshape(512, HD)

    def turned(part):
        return (part * cos + pltpu.roll(part, HD // 2, 1) * sin).astype(BF16)

    def finish_kv(hi, put):
        put(0, turned(acc_kv[hi, :, :HD]).reshape(4, 128, HD))
        put(1, acc_kv[hi, :, HD:].astype(BF16).reshape(4, 128, HD))

    def finish_q(hi, put):
        for head in range(4):
            cols = slice(head * HD, (head + 1) * HD)
            put(cols, turned(acc_q[hi, :, cols]).reshape(4, 128, HD))

    def put_kv_out(i, value):
        kv_out[i] = value

    def put_q_out(cols, value):
        q_out[:, :, cols] = value

    def put_kv(i, value):
        (k_ref, v_ref)[i][:, y_hi] = value

    def put_q(cols, value):
        q_ref[:, y_hi, :, cols] = value

    finish_kv(1 - y_hi, put_kv_out)
    send("kv", kv_out, at(dy=2), kv_in)
    finish_q(1 - y_hi, put_q_out)
    send("q", q_out, at(dy=2), q_in)
    finish_kv(y_hi, put_kv)
    finish_q(y_hi, put_q)
    arrived("kv")
    k_ref[:, 1 - y_hi] = kv_in[0]
    v_ref[:, 1 - y_hi] = kv_in[1]
    arrived("q")
    q_ref[:, 1 - y_hi] = q_in[...]
    for copy in started:
        copy.wait_send()


def rope_tables(cart, seq):
    frequency = np.power(np.float32(ROPE_BASE), np.arange(HD // 2, dtype=np.float32) * np.float32(-2.0 / HD))
    angles = (cart + np.arange(seq, dtype=np.float32))[:, None] * frequency.astype(np.float32)[None, :]
    cos, sin = np.cos(angles), np.sin(angles)
    shape = (seq // 256, 2, 128, HD)
    return (
        np.concatenate([cos, cos], axis=1).astype(np.float32).reshape(shape),
        np.concatenate([-sin, sin], axis=1).astype(np.float32).reshape(shape),
    )


def project(hidden, gain, w_query, w_keyval, cart):
    vmem, hbm = pl.BlockSpec(memory_space=pltpu.VMEM), pl.BlockSpec(memory_space=pl.ANY)
    cos, sin = rope_tables(cart, 1024)
    copies = 160
    q, k, v = pl.pallas_call(
        project_kernel,
        name="project",
        out_shape=(
            jax.ShapeDtypeStruct((4, 2, 128, 512), BF16),
            jax.ShapeDtypeStruct((4, 2, 128, HD), BF16),
            jax.ShapeDtypeStruct((4, 2, 128, HD), BF16),
        ),
        in_specs=[vmem, vmem, hbm, hbm, vmem, vmem],
        out_specs=(vmem,) * 3,
        scratch_shapes=[
            pltpu.VMEM((2, 8, 4, 128, 256), BF16),
            pltpu.VMEM((2, 2, 8, 2, 128, 512), BF16),
            pltpu.VMEM((2, 2, 8, 2, 128, 256), BF16),
            pltpu.VMEM((2, 512, 512), F32),
            pltpu.VMEM((2, 512, 256), F32),
            pltpu.VMEM((4, 128, 512), BF16),
            pltpu.VMEM((2, 4, 128, HD), BF16),
            pltpu.VMEM((4, 128, 512), BF16),
            pltpu.VMEM((2, 4, 128, HD), BF16),
            pltpu.SemaphoreType.DMA((2,)),
            pltpu.SemaphoreType.DMA((copies,)),
            pltpu.SemaphoreType.DMA((copies,)),
        ],
        compiler_params=pltpu.CompilerParams(collective_id=0, has_side_effects=True, vmem_limit_bytes=48 << 20),
    )(hidden, gain.reshape(1, -1), w_query, w_keyval.reshape(128, 256), cos, sin)
    return q.reshape(1024, 512), k.reshape(1024, HD), v.reshape(1024, HD)


def attention_kernel(len_ref, q_ref, kn_ref, vn_ref, cart_ref, g_ref, o_ref, grad_ref, kx, vt):
    length = len_ref[0]
    cart = cart_ref.shape[1]
    seq = kn_ref.shape[0]
    heads = q_ref.shape[1] // HD
    scale = HD ** -0.5
    factor = scale * math.log2(math.e)
    nt = (((1,), (1,)), ((), ()))

    live = lax.broadcasted_iota(jnp.int32, (seq, HD), 0) < length
    kx[:cart] = cart_ref[0]
    kx[cart:] = jnp.where(live, kn_ref[...], jnp.broadcast_to(cart_ref[0, 0:1, :], (seq, HD)))
    vt[:HD, :cart] = cart_ref[1].astype(F32).T.astype(BF16)
    vt[:HD, cart:] = jnp.where(live, vn_ref[...].astype(F32), 0.0).T.astype(BF16)
    extra = vt.shape[0] - HD
    spot = lax.broadcasted_iota(jnp.int32, (extra, cart + seq), 1)
    vt[HD:] = jnp.where(spot < cart + length, 1.0, 0.0).astype(BF16)
    grad_ref[...] = jnp.zeros_like(grad_ref)

    for block in range(seq // ROWS):
        before = cart + block * ROWS
        rows = pl.ds(block * ROWS, ROWS)

        @pl.loop(0, heads)
        def _(head):
            columns = pl.ds(pl.multiple_of(head * HD, HD), HD)
            q = q_ref[rows, columns]
            g = g_ref[rows, columns]
            row = block * ROWS + lax.broadcasted_iota(jnp.int32, (ROWS, HD), 0)
            g = jnp.where(row < length, g, jnp.zeros_like(g))
            s_far = lax.dot_general(kx[:before], q, nt, preferred_element_type=F32)
            s_near = lax.dot_general(kx[before:before + ROWS], q, nt, preferred_element_type=F32)
            key = lax.broadcasted_iota(jnp.int32, (ROWS, ROWS), 0)
            query = lax.broadcasted_iota(jnp.int32, (ROWS, ROWS), 1)
            s_near = jnp.where(key <= query, s_near, -jnp.inf)
            top = jnp.maximum(
                jnp.max(s_far, axis=0, keepdims=True), jnp.max(s_near, axis=0, keepdims=True)
            )
            e_far = jnp.exp2((s_far - top) * factor)
            e_near = jnp.exp2((s_near - top) * factor)
            out = jnp.dot(vt[:, :before], e_far.astype(BF16), preferred_element_type=F32)
            out += jnp.dot(vt[:, before:before + ROWS], e_near.astype(BF16), preferred_element_type=F32)
            inverse = 1.0 / out[HD:HD + 1]
            out = out[:HD] * inverse
            o_ref[rows, columns] = out.T.astype(BF16)
            delta = jnp.sum(out * g.astype(F32).T, axis=0, keepdims=True)
            d_prob = lax.dot_general(cart_ref[1], g, nt, preferred_element_type=F32)
            prob = e_far[:cart] * inverse
            d_score = prob * (d_prob - delta)
            grad_ref[1] += jnp.dot(prob.astype(BF16), g, preferred_element_type=F32)
            grad_ref[0] += jnp.dot(d_score.astype(BF16), q, preferred_element_type=F32)

    grad_ref[0] = grad_ref[0] * scale


def attention(length, q, k_new, v_new, cartridge, g):
    vmem = pl.BlockSpec(memory_space=pltpu.VMEM)
    cart, seq = cartridge.shape[1], q.shape[0]
    return pl.pallas_call(
        attention_kernel,
        name="attention",
        out_shape=(
            jax.ShapeDtypeStruct(q.shape, BF16),
            jax.ShapeDtypeStruct((2, cart, HD), F32),
        ),
        in_specs=[pl.BlockSpec(memory_space=pltpu.SMEM)] + [vmem] * 5,
        out_specs=(vmem, vmem),
        scratch_shapes=[
            pltpu.VMEM((cart + seq, HD), BF16),
            pltpu.VMEM((HD + 16, cart + seq), BF16),
        ],
        compiler_params=pltpu.CompilerParams(vmem_limit_bytes=40 << 20),
    )(length, q, k_new, v_new, cartridge, g)


def reduce_kernel(chips, part_ref, sum_ref, from_core, half, to_chips, from_chips, mine, gathered, other,
                  core_send, core_recv, rs_send, rs_recv, ag_send, ag_recv):
    dp, fsdp = lax.axis_index("dp"), lax.axis_index("fsdp")
    chip, core = dp // 2, dp % 2
    rows = part_ref.shape[0] // 2
    share = rows // chips
    sibling = (chip * 2 + (1 - core), fsdp)

    def peer(step):
        return lax.rem(chip + step, chips)

    barrier = pltpu.get_barrier_semaphore()
    pl.semaphore_signal(barrier, inc=1, device_id=sibling, device_id_type=MESH)
    for step in range(1, chips):
        pl.semaphore_signal(barrier, inc=1, device_id=(peer(step) * 2 + core, fsdp), device_id_type=MESH)
    pl.semaphore_wait(barrier, chips)

    def send(src, dst, send_sem, recv_sem, target):
        copy = pltpu.make_async_remote_copy(
            src_ref=src, dst_ref=dst, send_sem=send_sem, recv_sem=recv_sem,
            device_id=target, device_id_type=MESH,
        )
        copy.start()
        return copy

    theirs = pl.ds(pl.multiple_of((1 - core) * rows, rows), rows)
    ours = pl.ds(pl.multiple_of(core * rows, rows), rows)
    copy = send(part_ref.at[theirs], from_core, core_send.at[0], core_recv.at[0], sibling)
    copy.wait()
    half[...] = (part_ref[ours] + from_core[...]).reshape(half.shape)
    to_chips[...] = half[...].astype(BF16)
    copies = [
        send(to_chips.at[peer(step)], from_chips.at[step], rs_send.at[step], rs_recv.at[step],
             (peer(step) * 2 + core, fsdp))
        for step in range(1, chips)
    ]
    total = half[chip]
    for step, copy in zip(range(1, chips), copies):
        copy.wait()
        total += from_chips[step].astype(F32)
    mine[...] = total.astype(BF16)
    gathered[chip] = total.astype(BF16)
    copies = [
        send(mine, gathered.at[chip], ag_send.at[step], ag_recv.at[step], (peer(step) * 2 + core, fsdp))
        for step in range(1, chips)
    ]
    for copy in copies:
        copy.wait()
    copy = send(gathered, other, core_send.at[1], core_recv.at[1], sibling)
    sum_ref[ours] = gathered[...].astype(F32).reshape(rows, HD)
    copy.wait()
    sum_ref[theirs] = other[...].astype(F32).reshape(rows, HD)


def reduce_over_dp(part, n_dp):
    chips = n_dp // 2
    rows = part.shape[0]
    share = rows // 2 // chips
    vmem = pl.BlockSpec(memory_space=pltpu.VMEM)
    dma = pltpu.SemaphoreType.DMA
    return pl.pallas_call(
        functools.partial(reduce_kernel, chips),
        name="reduce_over_dp",
        out_shape=jax.ShapeDtypeStruct(part.shape, F32),
        in_specs=[vmem],
        out_specs=vmem,
        scratch_shapes=[
            pltpu.VMEM((rows // 2, HD), F32),
            pltpu.VMEM((chips, share, HD), F32),
            pltpu.VMEM((chips, share, HD), BF16),
            pltpu.VMEM((chips, share, HD), BF16),
            pltpu.VMEM((share, HD), BF16),
            pltpu.VMEM((chips, share, HD), BF16),
            pltpu.VMEM((chips, share, HD), BF16),
            dma((2,)), dma((2,)), dma((chips,)), dma((chips,)), dma((chips,)), dma((chips,)),
        ],
        compiler_params=pltpu.CompilerParams(collective_id=1, has_side_effects=True),
    )(part)


def on_device(n_dp, hidden_in, lengths, cartridge, norm_gain, w_query, w_keyval, cotangent):
    cart = cartridge.shape[1]
    query, key_new, value_new = project(hidden_in, norm_gain, w_query, w_keyval, cart)
    mixed, part = attention(lengths, query, key_new, value_new, cartridge, cotangent)
    summed = reduce_over_dp(part.reshape(-1, HD), n_dp)
    return mixed, summed.reshape(2, cart, HD)


def solution(mesh):
    in_specs = (
        P(("dp", "fsdp"), None),
        P("dp"),
        P(None, None, "fsdp"),
        P(),
        P("dp", "fsdp"),
        P("dp", None, "fsdp"),
        P("dp", "fsdp"),
    )
    out_specs = (P("dp", "fsdp"), P(None, None, "fsdp"))
    return jax.shard_map(
        functools.partial(on_device, mesh.shape["dp"]),
        mesh=mesh, in_specs=in_specs, out_specs=out_specs, check_vma=False,
    )
```

```python
import functools
import math

import jax
import jax.numpy as jnp
import numpy as np
from jax import lax
from jax.experimental import pallas as pl
from jax.experimental.pallas import tpu as pltpu
from jax.sharding import PartitionSpec as P

HD = 128
MESH = pl.DeviceIdType.MESH
EPS = 1e-05
ROPE_BASE = 500000.0
F32 = jnp.float32
BF16 = jnp.bfloat16
NT = (((1,), (1,)), ((), ()))
CHIPS = 16


def layer_kernel(len_ref, hidden_hbm, gain_hbm, wq_ref, wkv_ref, cos_hbm, sin_hbm, cart_hbm, g_hbm,
                 mixed_ref, sum_ref,
                 hidden_ref, gain_ref, cos_ref, sin_ref, cart_ref, g_ref,
                 xn, wq, wkv, acc_q, acc_kv, q_out, kv_out, q_in, kv_in, q_own, kv_own,
                 kx, vt, e_keep, d_keep, top_keep, grad, from_core, half, to_chips, from_chips, gathered, other,
                 local_sem, send_sem, recv_sem):
    dp, fsdp = lax.axis_index("dp"), lax.axis_index("fsdp")
    x, y_hi, y_lo, z, c = fsdp // 2, fsdp % 2, dp // 16, (dp // 2) % 8, dp % 2
    chip = dp // 2
    y = y_hi * 2 + y_lo
    turn = 1 - 2 * c
    length = len_ref[0]
    cart, seq = cart_ref.shape[1], 1024
    scale = HD ** -0.5
    factor = scale * math.log2(math.e)

    def at(dx=0, dy=0, dz=0, other=False):
        yy = lax.rem(y + dy + 8, 4)
        return (
            lax.rem(yy, 2) * 16 + lax.rem(z + dz + 16, 8) * 2 + (1 - c if other else c),
            lax.rem(x + dx + 8, 4) * 2 + yy // 2,
        )

    def peer(step):
        return lax.rem(chip + step, CHIPS)

    def zs(r):
        return lax.rem(z + r + 16, 8)

    def ys(dy):
        yy = lax.rem(y + dy + 8, 4)
        return yy // 2, lax.rem(yy, 2)

    def xs(dx):
        return lax.rem(x + dx + 8, 4)

    slots, started = {}, []

    def send(name, ref, target, dst=None):
        assert name not in slots
        copy = pltpu.make_async_remote_copy(
            src_ref=ref, dst_ref=ref if dst is None else dst,
            send_sem=send_sem.at[len(started)], recv_sem=recv_sem.at[len(started)],
            device_id=target, device_id_type=MESH,
        )
        copy.start()
        slots[name] = copy
        started.append(copy)

    def arrived(name):
        slots[name].wait_recv()

    def wq_at(dy, r, core=None):
        hi, lo = ys(dy)
        return wq.at[hi, lo, zs(r), c if core is None else core]

    def wkv_at(dy, r):
        hi, lo = ys(dy)
        return wkv.at[hi, lo, zs(r), c]

    local = []
    for n, (ref, dst) in enumerate([
        (wq_ref, wq_at(0, 0)), (wkv_ref, wkv_at(0, 0)), (hidden_hbm, hidden_ref), (gain_hbm, gain_ref),
        (cos_hbm.at[:, y_hi], cos_ref), (sin_hbm.at[:, y_hi], sin_ref), (cart_hbm, cart_ref), (g_hbm, g_ref),
    ]):
        copy = pltpu.make_async_copy(ref, dst, local_sem.at[n])
        copy.start()
        local.append(copy)
    barrier = pltpu.get_barrier_semaphore()
    partners = [at(dx=1), at(dx=-1), at(dy=1), at(dy=-1), at(dy=2), at(dz=1), at(dz=-1), at(other=True)]
    peers = [(peer(step) * 2 + c, fsdp) for step in range(1, CHIPS)]
    for partner in partners + peers:
        pl.semaphore_signal(barrier, inc=1, device_id=partner, device_id_type=MESH)
    pl.semaphore_wait(barrier, len(partners) + len(peers))
    local[0].wait()
    local[1].wait()

    def ticks(i):
        return {0: [0], 4: [4]}.get(i, [i, -i])

    def wq_from_z(i):
        if i == 4:
            arrived(("zq", 4, 0))
            arrived(("zq", 4, 1))
        elif i:
            arrived(("zq", i))
            arrived(("zq", -i))
        if i < 3:
            send(("zq", i + 1), wq_at(0, i), at(dz=-1))
            send(("zq", -i - 1), wq_at(0, -i), at(dz=1))
        elif i == 3:
            send(("zq", 4, 0), wq_at(0, 3).at[pl.ds(0, 64)], at(dz=-1))
            send(("zq", 4, 1), wq_at(0, -3).at[pl.ds(64, 64)], at(dz=1))
        for r in ticks(i):
            send(("yq", -1, r), wq_at(0, r), at(dy=1))
            send(("yq", 1, r), wq_at(0, r), at(dy=-1))

    def wq_from_y(i):
        for r in ticks(i):
            arrived(("yq", -1, r))
            arrived(("yq", 1, r))
            way = turn if r in (0, 4) else (1 if r > 0 else -1)
            send(("yq", 2, r), wq_at(way, r), at(dy=-way))

    def wq_to_core(i):
        for r in ticks(i):
            arrived(("yq", 2, r))
            send(("cq", r), wq.at[:, :, zs(r), c], at(other=True))

    def wkv_from_z(i):
        if i == 4:
            arrived(("zk", 4, 0))
            arrived(("zk", 4, 1))
        elif i:
            arrived(("zk", i))
            arrived(("zk", -i))
        if i < 3:
            send(("zk", i + 1), wkv.at[:, :, zs(i), c], at(dz=-1))
            send(("zk", -i - 1), wkv.at[:, :, zs(-i), c], at(dz=1))
        elif i == 3:
            send(("zk", 4, 0), wkv.at[0, :, zs(3), c], at(dz=-1))
            send(("zk", 4, 1), wkv.at[1, :, zs(-3), c], at(dz=1))
        for r in ticks(i):
            send(("ck", r), wkv.at[:, :, zs(r), c], at(other=True))

    def rows_out(i):
        for r in ticks(i):
            send(("x", -1, r), xn.at[:, zs(r), x], at(dx=1))
            send(("x", 1, r), xn.at[:, zs(r), x], at(dx=-1))

    def rows_on(i):
        for r in ticks(i):
            arrived(("x", -1, r))
            arrived(("x", 1, r))
            send(("x", 2, r, 0), xn.at[0, zs(r), xs(1)], at(dx=-1))
            send(("x", 2, r, 1), xn.at[1, zs(r), xs(-1)], at(dx=1))

    def multiply(i, halves=(0, 1)):
        for r in ticks(i):
            arrived(("cq", r))
            arrived(("ck", r))
            arrived(("x", 2, r, 0))
            arrived(("x", 2, r, 1))
        for r in ticks(i):
            spot = zs(r)
            left = jnp.concatenate([xn[lo, spot].reshape(512, 256) for lo in range(2)], axis=1)
            for hi in range(2):
                right = jnp.concatenate([wq[hi, lo, spot].reshape(256, 512) for lo in range(2)], axis=0)
                term = jnp.dot(left, right, preferred_element_type=F32)
                acc_q[hi] = term if r == 0 else acc_q[hi] + term
                right = jnp.concatenate([wkv[hi, lo, spot].reshape(256, 256) for lo in range(2)], axis=0)
                term = jnp.dot(left, right, preferred_element_type=F32)
                acc_kv[hi] = term if r == 0 else acc_kv[hi] + term

    wq_from_z(0)
    send(("yk", -1), wkv_at(0, 0), at(dy=1))
    send(("yk", 1), wkv_at(0, 0), at(dy=-1))
    local[2].wait()
    local[3].wait()
    hidden = hidden_ref[...].astype(F32)
    inverse = lax.rsqrt(jnp.mean(hidden * hidden, axis=-1, keepdims=True) + EPS)
    for k in range(16):
        cols = slice(k * 256, (k + 1) * 256)
        part = hidden_ref[:, cols].astype(F32) * inverse * gain_ref[:, cols]
        xn[k // 8, k % 8, x] = part.astype(BF16)
    rows_out(0)
    rows_out(1)
    for copy in local[4:]:
        copy.wait()
    kx[:cart] = cart_ref[0]
    vt[:HD, :cart] = cart_ref[1].astype(F32).T.astype(BF16)
    spot = lax.broadcasted_iota(jnp.int32, (vt.shape[0] - HD, cart + seq), 1)
    vt[HD:] = jnp.where(spot < cart + length, 1.0, 0.0).astype(BF16)
    grad[...] = jnp.zeros_like(grad)
    arrived(("yk", -1))
    arrived(("yk", 1))
    send(("yk", 2), wkv_at(turn, 0), at(dy=-turn))
    wq_from_z(1)
    wq_from_y(0)
    rows_on(0)
    rows_out(2)
    arrived(("yk", 2))
    wkv_from_z(0)
    wq_to_core(0)
    wq_from_z(2)
    wq_from_y(1)
    rows_on(1)
    rows_out(3)
    multiply(0)
    wkv_from_z(1)
    wq_from_z(3)
    wq_to_core(1)
    wq_from_y(2)
    rows_on(2)
    rows_out(4)
    multiply(1)
    wkv_from_z(2)
    wq_from_z(4)
    wq_to_core(2)
    wq_from_y(3)
    rows_on(3)
    multiply(2)
    wkv_from_z(3)
    wq_to_core(3)
    wq_from_y(4)
    rows_on(4)
    multiply(3)
    wkv_from_z(4)
    wq_to_core(4)
    multiply(4)


    cos, sin = cos_ref[...].reshape(512, HD), sin_ref[...].reshape(512, HD)

    def turned(part):
        return (part * cos + pltpu.roll(part, HD // 2, 1) * sin).astype(BF16).reshape(4, HD, HD)

    def finish_kv(hi, out):
        out[0] = turned(acc_kv[hi, :, :HD])
        out[1] = acc_kv[hi, :, HD:].astype(BF16).reshape(4, HD, HD)

    theirs = 1 - y_hi
    finish_kv(theirs, kv_out)
    send("kv", kv_out, at(dy=2), kv_in)
    first_q = len(started)
    for head in range(4):
        q_out[head] = turned(acc_q[theirs, :, head * HD:(head + 1) * HD])
        send(("q", head), q_out.at[head], at(dy=2), q_in.at[head])
    for head in range(4):
        q_own[head] = turned(acc_q[y_hi, :, head * HD:(head + 1) * HD])

    def rows_of(hi):
        lane = lax.broadcasted_iota(jnp.int32, (1, 2 * HD), 1)
        return (lane // HD) * (2 * HD) + hi * HD + lax.rem(lane, HD)

    def grad_rows(head, j, hi):
        columns = pl.ds(pl.multiple_of(head * HD, HD), HD)
        g = g_ref[2 * j:2 * j + 2, hi, :, columns].reshape(2 * HD, HD)
        row = lax.broadcasted_iota(jnp.int32, (2 * HD, HD), 0)
        row = 4 * j * HD + (row // HD) * (2 * HD) + hi * HD + lax.rem(row, HD)
        return jnp.where(row < length, g, jnp.zeros_like(g))

    def cart_part(q, g):
        scores = lax.dot_general(kx[:cart], q, NT, preferred_element_type=F32)
        top = jnp.max(scores, axis=0, keepdims=True)
        d_prob = lax.dot_general(cart_ref[1], g, NT, preferred_element_type=F32)
        return jnp.exp2((scores - top) * factor), top, d_prob

    def new_part(head, j, hi, q, g, e_cart, top_cart, d_prob):
        near = cart + 4 * j * HD
        end = near + 4 * HD
        s_near = lax.dot_general(kx[near:end], q, NT, preferred_element_type=F32)
        key = lax.broadcasted_iota(jnp.int32, s_near.shape, 0)
        s_near = jnp.where(key <= rows_of(hi), s_near, -jnp.inf)
        top = jnp.maximum(top_cart, jnp.max(s_near, axis=0, keepdims=True))
        if j:
            s_far = lax.dot_general(kx[cart:near], q, NT, preferred_element_type=F32)
            top = jnp.maximum(top, jnp.max(s_far, axis=0, keepdims=True))
        shrink = jnp.exp2((top_cart - top) * factor)
        e_near = jnp.exp2((s_near - top) * factor).astype(BF16)
        out = jnp.dot(vt[:, :cart], e_cart.astype(BF16), preferred_element_type=F32) * shrink
        out += jnp.dot(vt[:, near:end], e_near, preferred_element_type=F32)
        if j:
            e_far = jnp.exp2((s_far - top) * factor).astype(BF16)
            out += jnp.dot(vt[:, cart:near], e_far, preferred_element_type=F32)
        inverse = 1.0 / out[HD:HD + 1]
        out = out[:HD] * inverse
        columns = pl.ds(pl.multiple_of(head * HD, HD), HD)
        mixed_ref[2 * j:2 * j + 2, hi, :, columns] = out.T.astype(BF16).reshape(2, HD, HD)
        delta = jnp.sum(out * g.astype(F32).T, axis=0, keepdims=True)
        prob = e_cart * (shrink * inverse)
        d_score = prob * (d_prob - delta)
        grad[1] += jnp.dot(prob.astype(BF16), g, preferred_element_type=F32)
        grad[0] += jnp.dot(d_score.astype(BF16), q, preferred_element_type=F32)

    @pl.loop(0, 4)
    def _(head):
        for j in range(2):
            q = q_own[head, 2 * j:2 * j + 2].reshape(2 * HD, HD)
            e_cart, top, d_prob = cart_part(q, grad_rows(head, j, y_hi))
            e_keep[head, j] = e_cart
            d_keep[head, j] = d_prob
            top_keep[head, j] = top

    finish_kv(y_hi, kv_own)
    arrived("kv")
    for n in range(4):
        for hi, blocks in ((y_hi, kv_own), (theirs, kv_in)):
            first = pl.multiple_of((2 * n + hi) * HD, HD)
            live = first + lax.broadcasted_iota(jnp.int32, (HD, HD), 0) < length
            spare = jnp.broadcast_to(cart_ref[0, 0:1, :], (HD, HD))
            kx[pl.ds(cart + first, HD)] = jnp.where(live, blocks[0, n], spare)
            values = jnp.where(live, blocks[1, n].astype(F32), 0.0)
            vt[:HD, pl.ds(cart + first, HD)] = values.T.astype(BF16)

    @pl.loop(0, 4)
    def _(head):
        for j in range(2):
            q = q_own[head, 2 * j:2 * j + 2].reshape(2 * HD, HD)
            g = grad_rows(head, j, y_hi)
            new_part(head, j, y_hi, q, g, e_keep[head, j], top_keep[head, j], d_keep[head, j])

    @pl.loop(0, 4)
    def _(head):
        pltpu.make_async_remote_copy(
            src_ref=q_out.at[head], dst_ref=q_in.at[head], send_sem=send_sem.at[first_q + head],
            recv_sem=recv_sem.at[first_q + head], device_id=at(dy=2), device_id_type=MESH,
        ).wait_recv()
        for j in range(2):
            q = q_in[head, 2 * j:2 * j + 2].reshape(2 * HD, HD)
            g = grad_rows(head, j, theirs)
            new_part(head, j, theirs, q, g, *cart_part(q, g))

    rows = cart
    grad[0] = grad[0] * scale
    send("core_sum", grad.at[1 - c], at(other=True), from_core)
    arrived("core_sum")
    half[...] = (grad[c] + from_core[...]).reshape(half.shape)
    to_chips[...] = half[...].astype(BF16)
    for step in range(1, CHIPS):
        send(("rs", step), to_chips.at[peer(step)], peers[step - 1], from_chips.at[step])
    total = half[chip]
    for step in range(1, CHIPS):
        arrived(("rs", step))
        total += from_chips[step].astype(F32)
    gathered[chip] = total.astype(BF16)
    for step in range(1, CHIPS):
        send(("ag", step), gathered.at[chip], peers[step - 1])
    for step in range(1, CHIPS):
        arrived(("ag", step))
    send("core_back", gathered, at(other=True), other)
    sum_ref[c] = gathered[...].reshape(rows, HD)
    arrived("core_back")
    sum_ref[1 - c] = other[...].reshape(rows, HD)
    for copy in started:
        copy.wait_send()


def rope_tables(cart, seq):
    frequency = np.power(np.float32(ROPE_BASE), np.arange(HD // 2, dtype=np.float32) * np.float32(-2.0 / HD))
    angles = (cart + np.arange(seq, dtype=np.float32))[:, None] * frequency.astype(np.float32)[None, :]
    cos, sin = np.cos(angles), np.sin(angles)
    shape = (seq // 256, 2, 128, HD)
    return (
        np.concatenate([cos, cos], axis=1).astype(np.float32).reshape(shape),
        np.concatenate([-sin, sin], axis=1).astype(np.float32).reshape(shape),
    )


def tail_kernel(mixed_ref, sum_ref, mixed_out, sum_out, sem):
    copy = pltpu.make_async_copy(mixed_ref, mixed_out, sem)
    copy.start()
    sum_out[...] = sum_ref[...].astype(F32)
    copy.wait()


def on_device(hidden_in, lengths, cartridge, norm_gain, w_query, w_keyval, cotangent):
    cart = cartridge.shape[1]
    vmem, hbm = pl.BlockSpec(memory_space=pltpu.VMEM), pl.BlockSpec(memory_space=pltpu.HBM)
    cos, sin = rope_tables(cart, 1024)
    copies, share = 200, cart // CHIPS
    mixed, summed = pl.pallas_call(
        layer_kernel,
        name="layer",
        out_shape=(
            jax.ShapeDtypeStruct((4, 2, 128, 512), BF16),
            jax.ShapeDtypeStruct((2, cart, HD), BF16),
        ),
        in_specs=[pl.BlockSpec(memory_space=pltpu.SMEM)] + [hbm] * 8,
        out_specs=(vmem,) * 2,
        scratch_shapes=[
            pltpu.VMEM((128, 4096), BF16),
            pltpu.VMEM((1, 4096), F32),
            pltpu.VMEM((4, 128, HD), F32),
            pltpu.VMEM((4, 128, HD), F32),
            pltpu.VMEM((2, cart, HD), BF16),
            pltpu.VMEM((4, 2, 128, 512), BF16),
            pltpu.VMEM((2, 8, 4, 128, 256), BF16),
            pltpu.VMEM((2, 2, 8, 2, 128, 512), BF16),
            pltpu.VMEM((2, 2, 8, 2, 128, 256), BF16),
            pltpu.VMEM((2, 512, 512), F32),
            pltpu.VMEM((2, 512, 256), F32),
            pltpu.VMEM((4, 4, 128, HD), BF16),
            pltpu.VMEM((2, 4, 128, HD), BF16),
            pltpu.VMEM((4, 4, 128, HD), BF16),
            pltpu.VMEM((2, 4, 128, HD), BF16),
            pltpu.VMEM((4, 4, 128, HD), BF16),
            pltpu.VMEM((2, 4, 128, HD), BF16),
            pltpu.VMEM((cart + 1024, HD), BF16),
            pltpu.VMEM((HD + 16, cart + 1024), BF16),
            pltpu.VMEM((4, 2, cart, 256), F32),
            pltpu.VMEM((4, 2, cart, 256), F32),
            pltpu.VMEM((4, 2, 1, 256), F32),
            pltpu.VMEM((2, cart, HD), F32),
            pltpu.VMEM((cart, HD), F32),
            pltpu.VMEM((CHIPS, share, HD), F32),
            pltpu.VMEM((CHIPS, share, HD), BF16),
            pltpu.VMEM((CHIPS, share, HD), BF16),
            pltpu.VMEM((CHIPS, share, HD), BF16),
            pltpu.VMEM((CHIPS, share, HD), BF16),
            pltpu.SemaphoreType.DMA((8,)),
            pltpu.SemaphoreType.DMA((copies,)),
            pltpu.SemaphoreType.DMA((copies,)),
        ],
        compiler_params=pltpu.CompilerParams(collective_id=0, has_side_effects=True, vmem_limit_bytes=60 << 20),
    )(lengths, hidden_in, norm_gain.reshape(1, -1), w_query, w_keyval.reshape(128, 256), cos, sin, cartridge,
      cotangent.reshape(4, 2, 128, 512))
    mixed, summed = pl.pallas_call(
        tail_kernel,
        name="tail",
        out_shape=(
            jax.ShapeDtypeStruct(mixed.shape, BF16),
            jax.ShapeDtypeStruct(summed.shape, F32),
        ),
        in_specs=[vmem, vmem],
        out_specs=(pl.BlockSpec(memory_space=pl.ANY), vmem),
        scratch_shapes=[pltpu.SemaphoreType.DMA],
    )(mixed, summed)
    return mixed.reshape(1024, 512), summed


def solution(mesh):
    in_specs = (
        P(("dp", "fsdp"), None),
        P("dp"),
        P(None, None, "fsdp"),
        P(),
        P("dp", "fsdp"),
        P("dp", None, "fsdp"),
        P("dp", "fsdp"),
    )
    out_specs = (P("dp", "fsdp"), P(None, None, "fsdp"))
    return jax.shard_map(on_device, mesh=mesh, in_specs=in_specs, out_specs=out_specs, check_vma=False)
```

```python
import functools
import math

import jax
import jax.numpy as jnp
import numpy as np
from jax import lax
from jax.experimental import pallas as pl
from jax.experimental.pallas import tpu as pltpu
from jax.sharding import PartitionSpec as P

HD = 128
MESH = pl.DeviceIdType.MESH
EPS = 1e-05
ROPE_BASE = 500000.0
F32 = jnp.float32
BF16 = jnp.bfloat16
NT = (((1,), (1,)), ((), ()))
CHIPS = 16
FAR_FIRST = sorted(range(1, CHIPS), key=lambda step: -min(step % 8, 8 - step % 8))
STEPS = (0, 1, -1, 2, -2, 3, -3, 4)
SLOT = {step: n for n, step in enumerate(STEPS)}
TICKS = ((0, 1), (1, 2), (3, 2), (5, 2), (7, 1))
X_PARTS = ((0, 3), (3, 2), (5, 3))
MAIN = 128

def layer_kernel(len_ref, hidden_hbm, gain_hbm, wq_ref, wkv_ref, cos_hbm, sin_hbm, cart_hbm, g_hbm,
                 mixed_ref, sum_ref,
                 hidden_ref, gain_ref, cos_ref, sin_ref, cart_ref, g_ref,
                 xn, wa, wb, acc_q, acc_kv, q_out, kv_out, q_in, kv_in, q_own, kv_own,
                 kx, vt, e_keep, d_keep, top_keep, grad, from_core, half, to_chips, from_chips, gathered, other,
                 local_sem, send_sem, recv_sem):
    dp, fsdp = lax.axis_index("dp"), lax.axis_index("fsdp")
    x, y_hi, y_lo, z, c = fsdp // 2, fsdp % 2, dp // 16, (dp // 2) % 8, dp % 2
    chip = dp // 2
    y = y_hi * 2 + y_lo
    turn = 1 - 2 * c
    length = len_ref[0]
    cart, seq = cart_ref.shape[1], 1024
    scale = HD ** -0.5
    factor = scale * math.log2(math.e)

    def at(dx=0, dy=0, dz=0, other=False):
        yy = lax.rem(y + dy + 8, 4)
        return (
            lax.rem(yy, 2) * 16 + lax.rem(z + dz + 16, 8) * 2 + (1 - c if other else c),
            lax.rem(x + dx + 8, 4) * 2 + yy // 2,
        )

    def peer(step):
        return lax.rem(chip + step, CHIPS)

    def ys(dy):
        yy = lax.rem(y + dy + 8, 4)
        return yy // 2, lax.rem(yy, 2)

    def xs(dx):
        return lax.rem(x + dx + 8, 4)

    slots, started = {}, []

    def send(name, ref, target, dst=None):
        assert name not in slots
        copy = pltpu.make_async_remote_copy(
            src_ref=ref, dst_ref=ref if dst is None else dst,
            send_sem=send_sem.at[len(started)], recv_sem=recv_sem.at[len(started)],
            device_id=target, device_id_type=MESH,
        )
        copy.start()
        slots[name] = copy
        started.append(copy)

    def arrived(name):
        slots[name].wait_recv()

    def main(dy, n, count=1):
        hi, lo = ys(dy)
        return wa.at[hi, lo, c, pl.ds(n, count)]

    def rest(dy, n):
        hi, lo = ys(dy)
        return wb.at[hi, lo, c, n]

    barrier = pltpu.get_barrier_semaphore()
    partners = [at(dx=1), at(dx=-1), at(dy=1), at(dy=-1), at(dy=2), at(dz=1), at(dz=-1), at(other=True)]
    peers = [(peer(step) * 2 + c, fsdp) for step in range(1, CHIPS)]
    for partner in partners + peers:
        pl.semaphore_signal(barrier, inc=1, device_id=partner, device_id_type=MESH)
    local = []
    for n, (ref, dst) in enumerate([
        (wkv_ref, rest(0, 0)),
        (wq_ref, wa.at[y_hi, y_lo, c, 0]),
        (hidden_hbm, hidden_ref), (gain_hbm, gain_ref),
        (cos_hbm.at[:, y_hi], cos_ref), (sin_hbm.at[:, y_hi], sin_ref), (cart_hbm, cart_ref), (g_hbm, g_ref),
    ]):
        copy = pltpu.make_async_copy(ref, dst, local_sem.at[n])
        copy.start()
        local.append(copy)
    pl.semaphore_wait(barrier, len(partners) + len(peers))
    for copy in local[:2]:
        copy.wait()

    def main_from_z(i):
        if i == 4:
            arrived(("za", 4, 1))
            arrived(("za", 4, -1))
        for way in (1, -1):
            if 0 < i < 4:
                arrived(("za", way * i))
            if i < 3:
                send(("za", way * (i + 1)), main(0, SLOT[way * i]), at(dz=-way), main(0, SLOT[way * (i + 1)]))
        if i == 3:
            for way, part in ((1, pl.ds(0, 64)), (-1, pl.ds(64, MAIN - 64))):
                send(("za", 4, way), main(0, SLOT[3 * way]).at[:, part], at(dz=-way), main(0, SLOT[4]).at[:, part])
        n, count = TICKS[i]
        for way in (1, -1):
            send(("ya", -way, i), main(0, n, count), at(dy=way))

    def main_from_y(i):
        n, count = TICKS[i]
        for way in (1, -1):
            arrived(("ya", way, i))
            if count == 2:
                ref = main(way, n + (1 - way) // 2)
            else:
                ref = main(way, n).at[:, pl.ds(0, 64) if way == 1 else pl.ds(64, MAIN - 64)]
            send(("ya", 2, way, i), ref, at(dy=-way))

    def main_to_core(i):
        n, count = TICKS[i]
        arrived(("ya", 2, 1, i))
        arrived(("ya", 2, -1, i))
        send(("ca", i), wa.at[:, :, c, pl.ds(n, count)], at(other=True))

    def rest_along_y():
        for way in (1, -1):
            send(("yb", -way), rest(0, 0), at(dy=way))

    def rest_further_along_y():
        for way in (1, -1):
            arrived(("yb", way))
            send(("yb", 2, way), rest(way, 0).at[pl.ds(0 if way == 1 else 64, 64)], at(dy=-way))

    def rest_from_z(i):
        if i == 0:
            arrived(("yb", 2, 1))
            arrived(("yb", 2, -1))
        for hi in range(2):
            if i == 4:
                arrived(("zb", 4, hi))
                continue
            for way in (1, -1):
                here = wb.at[hi, :, c, SLOT[way * i]]
                if i:
                    arrived(("zb", way * i, hi))
                if i < 3:
                    send(("zb", way * (i + 1), hi), here, at(dz=-way), wb.at[hi, :, c, SLOT[way * (i + 1)]])
                elif way == 1 - 2 * hi:
                    send(("zb", 4, hi), here, at(dz=-way), wb.at[hi, :, c, SLOT[4]])
        n, count = TICKS[i]
        send(("cb", i), wb.at[:, :, c, pl.ds(n, count)], at(other=True))

    def rows_out(part):
        n, count = X_PARTS[part]
        for way in (1, -1):
            send(("x", -way, part), xn.at[x, pl.ds(n, count)], at(dx=way))

    def rows_on(part):
        n, count = X_PARTS[part]
        for way in (1, -1):
            arrived(("x", way, part))
            send(("x", 2, way, part), xn.at[xs(way), pl.ds(n, count), (1 - way) // 2], at(dx=-way))

    def rows_ready(part):
        arrived(("x", 2, 1, part))
        arrived(("x", 2, -1, part))

    def multiply(n, hi):
        left = jnp.concatenate([xn[:, n, lo].reshape(512, 256) for lo in range(2)], axis=1)
        parts = [(lo, core) for lo in range(2) for core in range(2)]
        right = jnp.concatenate([wb[hi, lo, core, n] for lo, core in parts], axis=0)
        term = jnp.dot(left, right, preferred_element_type=F32)
        acc_kv[hi] = acc_kv[hi] + term if n else term
        right = jnp.concatenate([wa[hi, lo, core, n] for lo, core in parts], axis=0)
        term = jnp.dot(left, right, preferred_element_type=F32)
        acc_q[hi] = acc_q[hi] + term if n else term

    def ready(i):
        arrived(("ca", i))
        arrived(("cb", i))

    def multiply_all(i):
        ready(i)
        n, count = TICKS[i]
        for slot in range(n, n + count):
            for hi in range(2):
                multiply(slot, hi)

    rest_along_y()
    main_from_z(0)
    local[2].wait()
    local[3].wait()
    hidden = hidden_ref[...].astype(F32)
    inverse = lax.rsqrt(jnp.mean(hidden * hidden, axis=-1, keepdims=True) + EPS)
    for n, step in enumerate(STEPS):
        for lo in range(2):
            k = lo * 8 + lax.rem(z + step + 8, 8)
            cols = pl.ds(pl.multiple_of(k * 256, 256), 256)
            part = hidden_ref[:, cols].astype(F32) * inverse * gain_ref[:, cols]
            xn[x, n, lo] = part.astype(BF16)
    rows_out(0)
    rows_out(1)
    for copy in local[4:]:
        copy.wait()
    kx[:cart] = cart_ref[0]
    vt[:HD, :cart] = cart_ref[1].astype(F32).T.astype(BF16)
    spot = lax.broadcasted_iota(jnp.int32, (vt.shape[0] - HD, cart + seq), 1)
    vt[HD:] = jnp.where(spot < cart + length, 1.0, 0.0).astype(BF16)
    grad[...] = jnp.zeros_like(grad)
    rest_further_along_y()
    main_from_z(1)
    rest_from_z(0)
    main_from_y(0)
    main_from_z(2)
    rest_from_z(1)
    main_from_y(1)
    main_to_core(0)
    main_from_z(3)
    rows_on(0)
    rows_out(2)
    rest_from_z(2)
    main_from_y(2)
    main_to_core(1)
    main_from_z(4)
    rows_ready(0)
    multiply_all(0)
    rest_from_z(3)
    main_from_y(3)
    main_to_core(2)
    rows_on(1)
    multiply_all(1)
    main_from_y(4)
    main_to_core(3)
    rest_from_z(4)
    rows_on(2)
    rows_ready(1)
    multiply_all(2)
    main_to_core(4)
    rows_ready(2)
    multiply_all(3)
    ready(4)
    theirs = 1 - y_hi
    multiply(7, theirs)

    cos, sin = cos_ref[...].reshape(512, HD), sin_ref[...].reshape(512, HD)

    def turned(part):
        return (part * cos + pltpu.roll(part, HD // 2, 1) * sin).astype(BF16).reshape(4, HD, HD)

    def finish_kv(hi, out):
        out[0] = turned(acc_kv[hi, :, :HD])
        out[1] = acc_kv[hi, :, HD:].astype(BF16).reshape(4, HD, HD)

    first_kv = len(started)
    finish_kv(theirs, kv_out)
    send("kv", kv_out, at(dy=2), kv_in)
    first_q = len(started)
    for head in range(4):
        q_out[head] = turned(acc_q[theirs, :, head * HD:(head + 1) * HD])
        if head < 3:
            send(("q", head), q_out.at[head], at(dy=2), q_in.at[head])
    for j in (1, 0):
        blocks = pl.ds(2 * j, 2)
        send(("q", 3, j), q_out.at[3, blocks], at(dy=2), q_in.at[3, blocks])
    multiply(7, y_hi)
    for head in range(4):
        q_own[head] = turned(acc_q[y_hi, :, head * HD:(head + 1) * HD])

    def rows_of(hi):
        lane = lax.broadcasted_iota(jnp.int32, (1, 2 * HD), 1)
        return (lane // HD) * (2 * HD) + hi * HD + lax.rem(lane, HD)

    def grad_rows(head, j, hi):
        columns = pl.ds(pl.multiple_of(head * HD, HD), HD)
        g = g_ref[2 * j:2 * j + 2, hi, :, columns].reshape(2 * HD, HD)
        row = lax.broadcasted_iota(jnp.int32, (2 * HD, HD), 0)
        row = 4 * j * HD + (row // HD) * (2 * HD) + hi * HD + lax.rem(row, HD)
        return jnp.where(row < length, g, jnp.zeros_like(g))

    def cart_part(q, g):
        scores = lax.dot_general(kx[:cart], q, NT, preferred_element_type=F32)
        top = jnp.max(scores, axis=0, keepdims=True)
        d_prob = lax.dot_general(cart_ref[1], g, NT, preferred_element_type=F32)
        return jnp.exp2((scores - top) * factor), top, d_prob

    def attend(head, hi, js, qs, gs, carts):
        columns = pl.ds(pl.multiple_of(head * HD, HD), HD)
        near, far, outs = [], [], []
        for j, q in zip(js, qs):
            first = cart + 4 * j * HD
            near.append(lax.dot_general(kx[first:first + 4 * HD], q, NT, preferred_element_type=F32))
            far.append(lax.dot_general(kx[cart:first], q, NT, preferred_element_type=F32) if j else None)
        key = lax.broadcasted_iota(jnp.int32, (4 * HD, 2 * HD), 0)
        allowed = key <= rows_of(hi)
        for j, s_near, s_far, (e_cart, top_cart, _) in zip(js, near, far, carts):
            first = cart + 4 * j * HD
            s_near = jnp.where(allowed, s_near, -jnp.inf)
            top = jnp.maximum(top_cart, jnp.max(s_near, axis=0, keepdims=True))
            if j:
                top = jnp.maximum(top, jnp.max(s_far, axis=0, keepdims=True))
            shrink = jnp.exp2((top_cart - top) * factor)
            e_near = jnp.exp2((s_near - top) * factor).astype(BF16)
            out = jnp.dot(vt[:, :cart], e_cart.astype(BF16), preferred_element_type=F32) * shrink
            out += jnp.dot(vt[:, first:first + 4 * HD], e_near, preferred_element_type=F32)
            if j:
                e_far = jnp.exp2((s_far - top) * factor).astype(BF16)
                out += jnp.dot(vt[:, cart:first], e_far, preferred_element_type=F32)
            outs.append((out, shrink))
        probs, scores = [], []
        for j, g, (out, shrink), (e_cart, _, d_prob) in zip(js, gs, outs, carts):
            inverse = 1.0 / out[HD:HD + 1]
            out = out[:HD] * inverse
            mixed_ref[2 * j:2 * j + 2, hi, :, columns] = out.T.astype(BF16).reshape(2, HD, HD)
            delta = jnp.sum(out * g.astype(F32).T, axis=0, keepdims=True)
            prob = e_cart * (shrink * inverse)
            scores.append((prob * (d_prob - delta)).astype(BF16))
            probs.append(prob.astype(BF16))
        join = functools.partial(jnp.concatenate, axis=0)
        grad[1] += jnp.dot(jnp.concatenate(probs, axis=1), join(gs), preferred_element_type=F32)
        grad[0] += jnp.dot(jnp.concatenate(scores, axis=1), join(qs), preferred_element_type=F32)

    def pairs(q_ref, head, hi, js=(0, 1)):
        qs = [q_ref[head, 2 * j:2 * j + 2].reshape(2 * HD, HD) for j in js]
        return qs, [grad_rows(head, j, hi) for j in js]

    @pl.loop(0, 4)
    def _(head):
        qs, gs = pairs(q_own, head, y_hi)
        for j in range(2):
            e_cart, top, d_prob = cart_part(qs[j], gs[j])
            e_keep[head, j] = e_cart
            d_keep[head, j] = d_prob
            top_keep[head, j] = top

    finish_kv(y_hi, kv_own)
    for copy in started[:first_kv]:
        copy.wait_send()
    arrived("kv")
    for n in range(4):
        for hi, blocks in ((y_hi, kv_own), (theirs, kv_in)):
            first = pl.multiple_of((2 * n + hi) * HD, HD)
            live = first + lax.broadcasted_iota(jnp.int32, (HD, HD), 0) < length
            spare = jnp.broadcast_to(cart_ref[0, 0:1, :], (HD, HD))
            kx[pl.ds(cart + first, HD)] = jnp.where(live, blocks[0, n], spare)
            values = jnp.where(live, blocks[1, n].astype(F32), 0.0)
            vt[:HD, pl.ds(cart + first, HD)] = values.T.astype(BF16)

    @pl.loop(0, 4)
    def _(head):
        qs, gs = pairs(q_own, head, y_hi)
        kept = [(e_keep[head, j], top_keep[head, j], d_keep[head, j]) for j in range(2)]
        attend(head, y_hi, (0, 1), qs, gs, kept)

    @pl.loop(0, 3)
    def _(head):
        pltpu.make_async_remote_copy(
            src_ref=q_out.at[head], dst_ref=q_in.at[head], send_sem=send_sem.at[first_q + head],
            recv_sem=recv_sem.at[first_q + head], device_id=at(dy=2), device_id_type=MESH,
        ).wait_recv()
        qs, gs = pairs(q_in, head, theirs)
        attend(head, theirs, (0, 1), qs, gs, [cart_part(q, g) for q, g in zip(qs, gs)])

    for j in (1, 0):
        arrived(("q", 3, j))
        qs, gs = pairs(q_in, 3, theirs, (j,))
        attend(3, theirs, (j,), qs, gs, [cart_part(qs[0], gs[0])])

    rows = cart
    send("core_sum", grad.at[1 - c], at(other=True), from_core)
    arrived("core_sum")
    half[...] = (grad[c] + from_core[...]).reshape(half.shape)
    to_chips[...] = half[...].astype(BF16)
    for step in FAR_FIRST:
        send(("rs", step), to_chips.at[peer(step)], peers[step - 1], from_chips.at[step])
    done = len(started)
    for copy in started[first_kv:]:
        copy.wait_send()
    total = half[chip]
    for step in reversed(FAR_FIRST):
        arrived(("rs", step))
        total += from_chips[step].astype(F32)
    total = total * jnp.where(c == 0, scale, 1.0)
    gathered[chip] = total.astype(BF16)
    for step in FAR_FIRST:
        send(("ag", step), gathered.at[chip], peers[step - 1])
    for step in range(1, CHIPS):
        arrived(("ag", step))
    send("core_back", gathered, at(other=True), other)
    sum_ref[c] = gathered[...].reshape(rows, HD)
    arrived("core_back")
    sum_ref[1 - c] = other[...].reshape(rows, HD)
    for copy in started[done:]:
        copy.wait_send()


def rope_tables(cart, seq):
    frequency = np.power(np.float32(ROPE_BASE), np.arange(HD // 2, dtype=np.float32) * np.float32(-2.0 / HD))
    angles = (cart + np.arange(seq, dtype=np.float32))[:, None] * frequency.astype(np.float32)[None, :]
    cos, sin = np.cos(angles), np.sin(angles)
    shape = (seq // 256, 2, 128, HD)
    return (
        np.concatenate([cos, cos], axis=1).astype(np.float32).reshape(shape),
        np.concatenate([-sin, sin], axis=1).astype(np.float32).reshape(shape),
    )


def tail_kernel(mixed_ref, sum_ref, mixed_out, sum_out):
    mixed_out[...] = mixed_ref[...]
    sum_out[...] = sum_ref[...].astype(F32)


def on_device(hidden_in, lengths, cartridge, norm_gain, w_query, w_keyval, cotangent):
    cart = cartridge.shape[1]
    vmem, hbm = pl.BlockSpec(memory_space=pltpu.VMEM), pl.BlockSpec(memory_space=pltpu.HBM)
    cos, sin = rope_tables(cart, 1024)
    copies, share = 120, cart // CHIPS
    mixed, summed = pl.pallas_call(
        layer_kernel,
        name="layer",
        out_shape=(
            jax.ShapeDtypeStruct((4, 2, 128, 512), BF16),
            jax.ShapeDtypeStruct((2, cart, HD), BF16),
        ),
        in_specs=[pl.BlockSpec(memory_space=pltpu.SMEM)] + [hbm] * 8,
        out_specs=(vmem,) * 2,
        scratch_shapes=[
            pltpu.VMEM((128, 4096), BF16),
            pltpu.VMEM((1, 4096), F32),
            pltpu.VMEM((4, 128, HD), F32),
            pltpu.VMEM((4, 128, HD), F32),
            pltpu.VMEM((2, cart, HD), BF16),
            pltpu.VMEM((4, 2, 128, 512), BF16),
            pltpu.VMEM((4, 8, 2, 128, 256), BF16),
            pltpu.VMEM((2, 2, 2, 8, MAIN, 512), BF16),
            pltpu.VMEM((2, 2, 2, 8, 128, 256), BF16),
            pltpu.VMEM((2, 512, 512), F32),
            pltpu.VMEM((2, 512, 256), F32),
            pltpu.VMEM((4, 4, 128, HD), BF16),
            pltpu.VMEM((2, 4, 128, HD), BF16),
            pltpu.VMEM((4, 4, 128, HD), BF16),
            pltpu.VMEM((2, 4, 128, HD), BF16),
            pltpu.VMEM((4, 4, 128, HD), BF16),
            pltpu.VMEM((2, 4, 128, HD), BF16),
            pltpu.VMEM((cart + 1024, HD), BF16),
            pltpu.VMEM((HD + 16, cart + 1024), BF16),
            pltpu.VMEM((4, 2, cart, 256), F32),
            pltpu.VMEM((4, 2, cart, 256), F32),
            pltpu.VMEM((4, 2, 1, 256), F32),
            pltpu.VMEM((2, cart, HD), F32),
            pltpu.VMEM((cart, HD), F32),
            pltpu.VMEM((CHIPS, share, HD), F32),
            pltpu.VMEM((CHIPS, share, HD), BF16),
            pltpu.VMEM((CHIPS, share, HD), BF16),
            pltpu.VMEM((CHIPS, share, HD), BF16),
            pltpu.VMEM((CHIPS, share, HD), BF16),
            pltpu.SemaphoreType.DMA((8,)),
            pltpu.SemaphoreType.DMA((copies,)),
            pltpu.SemaphoreType.DMA((copies,)),
        ],
        compiler_params=pltpu.CompilerParams(collective_id=0, has_side_effects=True, vmem_limit_bytes=60 << 20),
    )(lengths, hidden_in, norm_gain.reshape(1, -1), w_query, w_keyval.reshape(128, 256), cos, sin, cartridge,
      cotangent.reshape(4, 2, 128, 512))
    blocks = (
        pl.BlockSpec((2, 2, 128, 512), lambda i: (i, 0, 0, 0)),
        pl.BlockSpec((1, cart, HD), lambda i: (i, 0, 0)),
    )
    mixed, summed = pl.pallas_call(
        tail_kernel,
        name="tail",
        out_shape=(
            jax.ShapeDtypeStruct(mixed.shape, BF16),
            jax.ShapeDtypeStruct(summed.shape, F32),
        ),
        grid=(2,),
        in_specs=blocks,
        out_specs=blocks,
    )(mixed, summed)
    return mixed.reshape(1024, 512), summed


def solution(mesh):
    in_specs = (
        P(("dp", "fsdp"), None),
        P("dp"),
        P(None, None, "fsdp"),
        P(),
        P("dp", "fsdp"),
        P("dp", None, "fsdp"),
        P("dp", "fsdp"),
    )
    out_specs = (P("dp", "fsdp"), P(None, None, "fsdp"))
    return jax.shard_map(on_device, mesh=mesh, in_specs=in_specs, out_specs=out_specs, check_vma=False)
```

```python
import functools
import math

import jax
import jax.numpy as jnp
import numpy as np
from jax import lax
from jax.experimental import pallas as pl
from jax.experimental.pallas import tpu as pltpu
from jax.sharding import PartitionSpec as P

HD = 128
MESH = pl.DeviceIdType.MESH
EPS = 1e-05
ROPE_BASE = 500000.0
F32 = jnp.float32
BF16 = jnp.bfloat16
NT = (((1,), (1,)), ((), ()))
CHIPS = 16
FAR_FIRST = sorted(range(1, CHIPS), key=lambda step: -min(step % 8, 8 - step % 8))
STEPS = (0, 1, -1, 2, -2, 3, -3, 4)
SLOT = {step: n for n, step in enumerate(STEPS)}
TICKS = ((0, 1), (1, 2), (3, 2), (5, 2), (7, 1))
X_PARTS = ((0, 3), (3, 2), (5, 3))
MAIN = 128

def layer_kernel(len_ref, hidden_hbm, gain_hbm, wq_ref, wkv_ref, cos_hbm, sin_hbm, cart_hbm, g_hbm,
                 mixed_ref, sum_ref,
                 hidden_ref, gain_ref, cos_ref, sin_ref, cart_ref, g_ref,
                 xn, wa, wb, acc_q, acc_kv, q_out, kv_out, q_in, kv_in, q_own, kv_own,
                 k_new, vt_cart, vt_new, e_keep, d_keep, top_keep, out_keep, grad, from_core, half, to_chips, from_chips, gathered, other,
                 kv_rows, kv_wide, local_sem, send_sem, recv_sem):
    dp, fsdp = lax.axis_index("dp"), lax.axis_index("fsdp")
    x, y_hi, y_lo, z, c = fsdp // 2, fsdp % 2, dp // 16, (dp // 2) % 8, dp % 2
    chip = dp // 2
    y = y_hi * 2 + y_lo
    turn = 1 - 2 * c
    length = len_ref[0]
    cart, seq = cart_ref.shape[1], 1024
    scale = HD ** -0.5
    factor = scale * math.log2(math.e)

    def at(dx=0, dy=0, dz=0, other=False):
        yy = lax.rem(y + dy + 8, 4)
        return (
            lax.rem(yy, 2) * 16 + lax.rem(z + dz + 16, 8) * 2 + (1 - c if other else c),
            lax.rem(x + dx + 8, 4) * 2 + yy // 2,
        )

    def peer(step):
        return lax.rem(chip + step, CHIPS)

    def ys(dy):
        yy = lax.rem(y + dy + 8, 4)
        return yy // 2, lax.rem(yy, 2)

    def xs(dx):
        return lax.rem(x + dx + 8, 4)

    slots, started = {}, []

    def send(name, ref, target, dst=None):
        assert name not in slots
        copy = pltpu.make_async_remote_copy(
            src_ref=ref, dst_ref=ref if dst is None else dst,
            send_sem=send_sem.at[len(started)], recv_sem=recv_sem.at[len(started)],
            device_id=target, device_id_type=MESH,
        )
        copy.start()
        slots[name] = copy
        started.append(copy)

    def arrived(name):
        slots[name].wait_recv()

    def main(dy, n, count=1):
        hi, lo = ys(dy)
        return wa.at[hi, lo, c, pl.ds(n, count)]

    def rest(dy, n):
        hi, lo = ys(dy)
        return wb.at[hi, lo, c, n]

    barrier = pltpu.get_barrier_semaphore()
    partners = [at(dx=1), at(dx=-1), at(dy=1), at(dy=-1), at(dy=2), at(dz=1), at(dz=-1), at(other=True)]
    peers = [(peer(step) * 2 + c, fsdp) for step in range(1, CHIPS)]
    for partner in partners + peers:
        pl.semaphore_signal(barrier, inc=1, device_id=partner, device_id_type=MESH)
    local = []
    for n, (ref, dst) in enumerate([
        (wkv_ref, kv_rows),
        (wq_ref, wa.at[y_hi, y_lo, c, 0]),
        (hidden_hbm, hidden_ref), (gain_hbm, gain_ref),
        (cos_hbm.at[:, y_hi], cos_ref), (sin_hbm.at[:, y_hi], sin_ref), (cart_hbm, cart_ref), (g_hbm, g_ref),
    ]):
        copy = pltpu.make_async_copy(ref, dst, local_sem.at[n])
        copy.start()
        local.append(copy)
    local[0].wait()
    kv_wide[...] = kv_rows[...].astype(F32)
    for i in range(2):
        wb[y_hi, y_lo, c, 0, :, i * HD:(i + 1) * HD] = kv_wide[pl.ds(i, 128, 2)].astype(BF16)
    pl.semaphore_wait(barrier, len(partners) + len(peers))

    def main_from_z(i):
        if i == 4:
            arrived(("za", 4, 1))
            arrived(("za", 4, -1))
        for way in (1, -1):
            if 0 < i < 4:
                arrived(("za", way * i))
            if i < 3:
                ref = main(0, SLOT[way * i]).at[0] if i else wq_ref
                send(("za", way * (i + 1)), ref, at(dz=-way), main(0, SLOT[way * (i + 1)]).at[0])
        if i == 3:
            for way, part in ((1, pl.ds(0, 64)), (-1, pl.ds(64, MAIN - 64))):
                send(("za", 4, way), main(0, SLOT[3 * way]).at[:, part], at(dz=-way), main(0, SLOT[4]).at[:, part])
        n, count = TICKS[i]
        for slot in range(n, n + count):
            for way in (1, -1):
                ref = main(0, slot).at[0]
                send(("ya", -way, slot), ref if i else wq_ref, at(dy=way), ref)

    def main_from_y(i):
        n, count = TICKS[i]
        for way in (1, -1):
            slot = n + (1 - way) // 2 if count == 2 else n
            arrived(("ya", way, slot))
            ref = main(way, slot)
            if count == 1:
                ref = ref.at[:, pl.ds(0, 64) if way == 1 else pl.ds(64, MAIN - 64)]
            send(("ya", 2, way, i), ref, at(dy=-way))
        if count == 2:
            arrived(("ya", 1, n + 1))
            arrived(("ya", -1, n))

    def main_to_core(i):
        n, count = TICKS[i]
        arrived(("ya", 2, 1, i))
        arrived(("ya", 2, -1, i))
        send(("ca", i), wa.at[:, :, c, pl.ds(n, count)], at(other=True))

    def rest_along_y():
        for way in (1, -1):
            send(("yb", -way), rest(0, 0), at(dy=way))

    def rest_further_along_y():
        for way in (1, -1):
            arrived(("yb", way))
            send(("yb", 2, way), rest(way, 0).at[pl.ds(0 if way == 1 else 64, 64)], at(dy=-way))

    def rest_from_z(i):
        if i == 0:
            arrived(("yb", 2, 1))
            arrived(("yb", 2, -1))
        for hi in range(2):
            if i == 4:
                arrived(("zb", 4, hi))
                continue
            for way in (1, -1):
                here = wb.at[hi, :, c, SLOT[way * i]]
                if i:
                    arrived(("zb", way * i, hi))
                if i < 3:
                    send(("zb", way * (i + 1), hi), here, at(dz=-way), wb.at[hi, :, c, SLOT[way * (i + 1)]])
                elif way == 1 - 2 * hi:
                    send(("zb", 4, hi), here, at(dz=-way), wb.at[hi, :, c, SLOT[4]])
        n, count = TICKS[i]
        send(("cb", i), wb.at[:, :, c, pl.ds(n, count)], at(other=True))

    def rows_out(part):
        n, count = X_PARTS[part]
        for way in (1, -1):
            send(("x", -way, part), xn.at[x, pl.ds(n, count)], at(dx=way))

    def rows_on(part):
        n, count = X_PARTS[part]
        for way in (1, -1):
            arrived(("x", way, part))
            send(("x", 2, way, part), xn.at[xs(way), pl.ds(n, count), (1 - way) // 2], at(dx=-way))

    def rows_ready(part):
        arrived(("x", 2, 1, part))
        arrived(("x", 2, -1, part))

    def multiply(n, hi):
        left = jnp.concatenate([xn[:, n, lo].reshape(512, 256) for lo in range(2)], axis=1)
        parts = [(lo, core) for lo in range(2) for core in range(2)]
        right = jnp.concatenate([wb[hi, lo, core, n] for lo, core in parts], axis=0)
        term = jnp.dot(left, right, preferred_element_type=F32)
        acc_kv[hi] = acc_kv[hi] + term if n else term
        right = jnp.concatenate([wa[hi, lo, core, n] for lo, core in parts], axis=0)
        term = jnp.dot(left, right, preferred_element_type=F32)
        acc_q[hi] = acc_q[hi] + term if n else term

    def ready(i):
        arrived(("ca", i))
        arrived(("cb", i))

    def multiply_all(i):
        ready(i)
        n, count = TICKS[i]
        for slot in range(n, n + count):
            for hi in range(2):
                multiply(slot, hi)

    rest_along_y()
    main_from_z(0)
    local[1].wait()
    local[2].wait()
    local[3].wait()
    hidden = hidden_ref[...].astype(F32)
    inverse = lax.rsqrt(jnp.mean(hidden * hidden, axis=-1, keepdims=True) + EPS)
    for n, step in enumerate(STEPS):
        for lo in range(2):
            k = lo * 8 + lax.rem(z + step + 8, 8)
            cols = pl.ds(pl.multiple_of(k * 256, 256), 256)
            part = hidden_ref[:, cols].astype(F32) * inverse * gain_ref[:, cols]
            xn[x, n, lo] = part.astype(BF16)
    rows_out(0)
    rows_out(1)
    for copy in local[4:]:
        copy.wait()
    vt_cart[:HD] = cart_ref[1].astype(F32).T.astype(BF16)
    vt_cart[HD:] = jnp.ones((vt_cart.shape[0] - HD, cart), BF16)
    grad[...] = jnp.zeros_like(grad)
    rest_further_along_y()
    main_from_z(1)
    rest_from_z(0)
    main_from_y(0)
    main_from_z(2)
    rest_from_z(1)
    main_from_y(1)
    main_to_core(0)
    main_from_z(3)
    rows_on(0)
    rows_out(2)
    rest_from_z(2)
    main_from_y(2)
    main_to_core(1)
    main_from_z(4)
    rows_ready(0)
    multiply_all(0)
    rest_from_z(3)
    main_from_y(3)
    main_to_core(2)
    rows_on(1)
    multiply_all(1)
    main_from_y(4)
    main_to_core(3)
    rest_from_z(4)
    rows_on(2)
    rows_ready(1)
    multiply_all(2)
    main_to_core(4)
    rows_ready(2)
    multiply_all(3)
    ready(4)
    theirs = 1 - y_hi
    multiply(7, theirs)

    cos, sin = cos_ref[...].reshape(512, HD), sin_ref[...].reshape(512, HD)

    def turned(part):
        return (part * cos + pltpu.roll(part, HD // 2, 1) * sin).astype(BF16).reshape(4, HD, HD)

    def finish_kv(hi, out):
        out[0] = turned(acc_kv[hi, :, :HD])
        out[1] = acc_kv[hi, :, HD:].astype(BF16).reshape(4, HD, HD)

    first_kv = len(started)
    finish_kv(theirs, kv_out)
    send("kv", kv_out, at(dy=2), kv_in)
    first_q = len(started)
    for head in range(4):
        q_out[head] = turned(acc_q[theirs, :, head * HD:(head + 1) * HD])
        if head < 3:
            send(("q", head), q_out.at[head], at(dy=2), q_in.at[head])
    for j in (1, 0):
        blocks = pl.ds(2 * j, 2)
        send(("q", 3, j), q_out.at[3, blocks], at(dy=2), q_in.at[3, blocks])
    multiply(7, y_hi)
    for head in range(4):
        q_own[head] = turned(acc_q[y_hi, :, head * HD:(head + 1) * HD])

    def spots(hi, index):
        return (index // HD) * (2 * HD) + hi * HD + lax.rem(index, HD)

    def take_keys(hi, blocks):
        spare = jnp.broadcast_to(cart_ref[0, 0:1, :], (HD, HD))
        for n in range(4):
            live = spots(hi, n * HD + lax.broadcasted_iota(jnp.int32, (HD, HD), 0)) < length
            k_new[hi, n * HD:(n + 1) * HD] = jnp.where(live, blocks[0, n], spare)
            values = jnp.where(live, blocks[1, n].astype(F32), 0.0)
            vt_new[hi, :HD, n * HD:(n + 1) * HD] = values.T.astype(BF16)
        live = spots(hi, lax.broadcasted_iota(jnp.int32, (vt_new.shape[1] - HD, 4 * HD), 1)) < length
        vt_new[hi, HD:] = jnp.where(live, 1.0, 0.0).astype(BF16)

    def grad_rows(head, j, hi):
        columns = pl.ds(pl.multiple_of(head * HD, HD), HD)
        g = g_ref[2 * j:2 * j + 2, hi, :, columns].reshape(2 * HD, HD)
        row = lax.broadcasted_iota(jnp.int32, (2 * HD, HD), 0)
        row = 4 * j * HD + (row // HD) * (2 * HD) + hi * HD + lax.rem(row, HD)
        return jnp.where(row < length, g, jnp.zeros_like(g))

    def new_scores(key_hi, hi, j, q):
        near = lax.dot_general(k_new[key_hi, 2 * j * HD:2 * (j + 1) * HD], q, NT, preferred_element_type=F32)
        key = spots(key_hi, lax.broadcasted_iota(jnp.int32, near.shape, 0))
        row = spots(hi, lax.broadcasted_iota(jnp.int32, (1, 2 * HD), 1))
        near = jnp.where(key <= row, near, -jnp.inf)
        if j == 0:
            return [near]
        return [lax.dot_general(k_new[key_hi, :2 * j * HD], q, NT, preferred_element_type=F32), near]

    def highest(tops, scores):
        for part in scores:
            tops = jnp.maximum(tops, jnp.max(part, axis=0, keepdims=True))
        return tops

    def add_values(out, key_hi, scores, top):
        first = 0
        for part in scores:
            last = first + part.shape[0]
            weights = jnp.exp2((part - top) * factor).astype(BF16)
            out += jnp.dot(vt_new[key_hi, :, first:last], weights, preferred_element_type=F32)
            first = last
        return out

    def first_part(key_hi, hi, js, qs, gs):
        carts = [lax.dot_general(cart_ref[0], q, NT, preferred_element_type=F32) for q in qs]
        news = [new_scores(key_hi, hi, j, q) for j, q in zip(js, qs)]
        d_probs = [lax.dot_general(cart_ref[1], g, NT, preferred_element_type=F32) for g in gs]
        kept = []
        for scores, new, d_prob in zip(carts, news, d_probs):
            top = highest(jnp.max(scores, axis=0, keepdims=True), new)
            e_cart = jnp.exp2((scores - top) * factor)
            out = jnp.dot(vt_cart[...], e_cart.astype(BF16), preferred_element_type=F32)
            kept.append((e_cart, top, d_prob, add_values(out, key_hi, new, top)))
        return kept

    def second_part(head, key_hi, hi, js, qs, gs, kept):
        columns = pl.ds(pl.multiple_of(head * HD, HD), HD)
        news = [new_scores(key_hi, hi, j, q) for j, q in zip(js, qs)]
        outs = []
        for new, (_, before, _, out) in zip(news, kept):
            top = highest(before, new)
            shrink = jnp.exp2((before - top) * factor)
            outs.append((add_values(out * shrink, key_hi, new, top), shrink))
        probs, scores = [], []
        for j, g, (out, shrink), (e_cart, _, d_prob, _) in zip(js, gs, outs, kept):
            inverse = 1.0 / out[HD:HD + 1]
            out = out[:HD] * inverse
            mixed_ref[2 * j:2 * j + 2, hi, :, columns] = out.T.astype(BF16).reshape(2, HD, HD)
            delta = jnp.sum(out * g.astype(F32).T, axis=0, keepdims=True)
            prob = e_cart * (shrink * inverse)
            scores.append((prob * (d_prob - delta)).astype(BF16))
            probs.append(prob.astype(BF16))
        join = functools.partial(jnp.concatenate, axis=0)
        grad[1] += jnp.dot(jnp.concatenate(probs, axis=1), join(gs), preferred_element_type=F32)
        grad[0] += jnp.dot(jnp.concatenate(scores, axis=1), join(qs), preferred_element_type=F32)

    def pairs(q_ref, head, hi, js=(0, 1)):
        qs = [q_ref[head, 2 * j:2 * j + 2].reshape(2 * HD, HD) for j in js]
        return qs, [grad_rows(head, j, hi) for j in js]

    finish_kv(y_hi, kv_own)
    take_keys(y_hi, kv_own)
    both = (0, 1)

    @pl.loop(0, 4)
    def _(head):
        for j, kept in enumerate(first_part(y_hi, y_hi, both, *pairs(q_own, head, y_hi))):
            e_keep[head, j], top_keep[head, j], d_keep[head, j], out_keep[head, j] = kept

    for copy in started[:first_kv]:
        copy.wait_send()
    arrived("kv")
    take_keys(theirs, kv_in)

    @pl.loop(0, 4)
    def _(head):
        kept = [(e_keep[head, j], top_keep[head, j], d_keep[head, j], out_keep[head, j]) for j in both]
        second_part(head, theirs, y_hi, both, *pairs(q_own, head, y_hi), kept)

    @pl.loop(0, 3)
    def _(head):
        pltpu.make_async_remote_copy(
            src_ref=q_out.at[head], dst_ref=q_in.at[head], send_sem=send_sem.at[first_q + head],
            recv_sem=recv_sem.at[first_q + head], device_id=at(dy=2), device_id_type=MESH,
        ).wait_recv()
        qs, gs = pairs(q_in, head, theirs)
        second_part(head, theirs, theirs, both, qs, gs, first_part(y_hi, theirs, both, qs, gs))

    for j in (1, 0):
        arrived(("q", 3, j))
        qs, gs = pairs(q_in, 3, theirs, (j,))
        second_part(3, theirs, theirs, (j,), qs, gs, first_part(y_hi, theirs, (j,), qs, gs))

    rows = cart
    send("core_sum", grad.at[1 - c], at(other=True), from_core)
    arrived("core_sum")
    half[...] = (grad[c] + from_core[...]).reshape(half.shape)
    to_chips[...] = half[...].astype(BF16)
    for step in FAR_FIRST:
        send(("rs", step), to_chips.at[peer(step)], peers[step - 1], from_chips.at[step])
    done = len(started)
    for copy in started[first_kv:]:
        copy.wait_send()
    total = half[chip]
    for step in reversed(FAR_FIRST):
        arrived(("rs", step))
        total += from_chips[step].astype(F32)
    total = total * jnp.where(c == 0, scale, 1.0)
    gathered[chip] = total.astype(BF16)
    for step in FAR_FIRST:
        send(("ag", step), gathered.at[chip], peers[step - 1])
    for step in range(1, CHIPS):
        arrived(("ag", step))
    send("core_back", gathered, at(other=True), other)
    sum_ref[c] = gathered[...].reshape(rows, HD)
    arrived("core_back")
    sum_ref[1 - c] = other[...].reshape(rows, HD)
    for copy in started[done:]:
        copy.wait_send()


def rope_tables(cart, seq):
    frequency = np.power(np.float32(ROPE_BASE), np.arange(HD // 2, dtype=np.float32) * np.float32(-2.0 / HD))
    angles = (cart + np.arange(seq, dtype=np.float32))[:, None] * frequency.astype(np.float32)[None, :]
    cos, sin = np.cos(angles), np.sin(angles)
    shape = (seq // 256, 2, 128, HD)
    return (
        np.concatenate([cos, cos], axis=1).astype(np.float32).reshape(shape),
        np.concatenate([-sin, sin], axis=1).astype(np.float32).reshape(shape),
    )


def tail_kernel(mixed_ref, sum_ref, mixed_out, sum_out):
    mixed_out[...] = mixed_ref[...]
    sum_out[...] = sum_ref[...].astype(F32)


def on_device(hidden_in, lengths, cartridge, norm_gain, w_query, w_keyval, cotangent):
    cart = cartridge.shape[1]
    vmem, hbm = pl.BlockSpec(memory_space=pltpu.VMEM), pl.BlockSpec(memory_space=pltpu.HBM)
    cos, sin = rope_tables(cart, 1024)
    copies, share = 120, cart // CHIPS
    mixed, summed = pl.pallas_call(
        layer_kernel,
        name="layer",
        out_shape=(
            jax.ShapeDtypeStruct((4, 2, 128, 512), BF16),
            jax.ShapeDtypeStruct((2, cart, HD), BF16),
        ),
        in_specs=[pl.BlockSpec(memory_space=pltpu.SMEM)] + [hbm] * 8,
        out_specs=(vmem,) * 2,
        scratch_shapes=[
            pltpu.VMEM((128, 4096), BF16),
            pltpu.VMEM((1, 4096), F32),
            pltpu.VMEM((4, 128, HD), F32),
            pltpu.VMEM((4, 128, HD), F32),
            pltpu.VMEM((2, cart, HD), BF16),
            pltpu.VMEM((4, 2, 128, 512), BF16),
            pltpu.VMEM((4, 8, 2, 128, 256), BF16),
            pltpu.VMEM((2, 2, 2, 8, MAIN, 512), BF16),
            pltpu.VMEM((2, 2, 2, 8, 128, 256), BF16),
            pltpu.VMEM((2, 512, 512), F32),
            pltpu.VMEM((2, 512, 256), F32),
            pltpu.VMEM((4, 4, 128, HD), BF16),
            pltpu.VMEM((2, 4, 128, HD), BF16),
            pltpu.VMEM((4, 4, 128, HD), BF16),
            pltpu.VMEM((2, 4, 128, HD), BF16),
            pltpu.VMEM((4, 4, 128, HD), BF16),
            pltpu.VMEM((2, 4, 128, HD), BF16),
            pltpu.VMEM((2, 512, HD), BF16),
            pltpu.VMEM((HD + 16, cart), BF16),
            pltpu.VMEM((2, HD + 16, 512), BF16),
            pltpu.VMEM((4, 2, cart, 256), F32),
            pltpu.VMEM((4, 2, cart, 256), F32),
            pltpu.VMEM((4, 2, 1, 256), F32),
            pltpu.VMEM((4, 2, HD + 16, 256), F32),
            pltpu.VMEM((2, cart, HD), F32),
            pltpu.VMEM((cart, HD), F32),
            pltpu.VMEM((CHIPS, share, HD), F32),
            pltpu.VMEM((CHIPS, share, HD), BF16),
            pltpu.VMEM((CHIPS, share, HD), BF16),
            pltpu.VMEM((CHIPS, share, HD), BF16),
            pltpu.VMEM((CHIPS, share, HD), BF16),
            pltpu.VMEM((256, HD), BF16),
            pltpu.VMEM((256, HD), F32),
            pltpu.SemaphoreType.DMA((8,)),
            pltpu.SemaphoreType.DMA((copies,)),
            pltpu.SemaphoreType.DMA((copies,)),
        ],
        compiler_params=pltpu.CompilerParams(collective_id=0, has_side_effects=True, vmem_limit_bytes=60 << 20),
    )(lengths, hidden_in, norm_gain.reshape(1, -1), w_query, w_keyval.reshape(256, HD), cos, sin, cartridge,
      cotangent.reshape(4, 2, 128, 512))
    blocks = (
        pl.BlockSpec((2, 2, 128, 512), lambda i: (i, 0, 0, 0)),
        pl.BlockSpec((1, cart, HD), lambda i: (i, 0, 0)),
    )
    mixed, summed = pl.pallas_call(
        tail_kernel,
        name="tail",
        out_shape=(
            jax.ShapeDtypeStruct(mixed.shape, BF16),
            jax.ShapeDtypeStruct(summed.shape, F32),
        ),
        grid=(2,),
        in_specs=blocks,
        out_specs=blocks,
    )(mixed, summed)
    return mixed.reshape(1024, 512), summed


def solution(mesh):
    in_specs = (
        P(("dp", "fsdp"), None),
        P("dp"),
        P(None, None, "fsdp"),
        P(),
        P("dp", "fsdp"),
        P("dp", None, "fsdp"),
        P("dp", "fsdp"),
    )
    out_specs = (P("dp", "fsdp"), P(None, None, "fsdp"))
    return jax.shard_map(on_device, mesh=mesh, in_specs=in_specs, out_specs=out_specs, check_vma=False)
```

```python
import functools
import math

import jax
import jax.numpy as jnp
import numpy as np
from jax import lax
from jax.experimental import pallas as pl
from jax.experimental.pallas import tpu as pltpu
from jax.sharding import PartitionSpec as P

HD = 128
MESH = pl.DeviceIdType.MESH
EPS = 1e-05
ROPE_BASE = 500000.0
F32 = jnp.float32
BF16 = jnp.bfloat16
NT = (((1,), (1,)), ((), ()))
CHIPS = 16
FAR_FIRST = sorted(range(1, CHIPS), key=lambda step: -min(step % 8, 8 - step % 8))
STEPS = (0, 1, -1, 2, -2, 3, -3, 4)
SLOT = {step: n for n, step in enumerate(STEPS)}
TICKS = ((0, 1), (1, 2), (3, 2), (5, 2), (7, 1))
X_PARTS = ((0, 3), (3, 2), (5, 3))
MAIN = 128

def layer_kernel(len_ref, hidden_hbm, gain_hbm, wq_ref, wkv_ref, cos_hbm, sin_hbm, cart_hbm, g_hbm,
                 mixed_ref, sum_ref,
                 hidden_ref, gain_ref, cos_ref, sin_ref, cart_ref, g_ref,
                 xn, wa, wb, acc_q, acc_kv, q_out, kv_out, q_in, kv_in, q_own, kv_own,
                 k_new, vt_cart, vt_new, e_keep, d_keep, top_keep, out_keep, grad, from_core, half, to_chips, from_chips, gathered, other,
                 kv_rows, kv_wide, local_sem, send_sem, recv_sem):
    dp, fsdp = lax.axis_index("dp"), lax.axis_index("fsdp")
    x, y_hi, y_lo, z, c = fsdp // 2, fsdp % 2, dp // 16, (dp // 2) % 8, dp % 2
    chip = dp // 2
    y = y_hi * 2 + y_lo
    turn = 1 - 2 * c
    length = len_ref[0]
    cart, seq = cart_ref.shape[1], 1024
    scale = HD ** -0.5
    factor = scale * math.log2(math.e)

    def at(dx=0, dy=0, dz=0, other=False):
        yy = lax.rem(y + dy + 8, 4)
        return (
            lax.rem(yy, 2) * 16 + lax.rem(z + dz + 16, 8) * 2 + (1 - c if other else c),
            lax.rem(x + dx + 8, 4) * 2 + yy // 2,
        )

    def peer(step):
        return lax.rem(chip + step, CHIPS)

    def ys(dy):
        yy = lax.rem(y + dy + 8, 4)
        return yy // 2, lax.rem(yy, 2)

    def xs(dx):
        return lax.rem(x + dx + 8, 4)

    slots, started = {}, []

    def send(name, ref, target, dst=None):
        assert name not in slots
        copy = pltpu.make_async_remote_copy(
            src_ref=ref, dst_ref=ref if dst is None else dst,
            send_sem=send_sem.at[len(started)], recv_sem=recv_sem.at[len(started)],
            device_id=target, device_id_type=MESH,
        )
        copy.start()
        slots[name] = copy
        started.append(copy)

    def arrived(name):
        slots[name].wait_recv()

    def main(dy, n, count=1):
        hi, lo = ys(dy)
        return wa.at[hi, lo, c, pl.ds(n, count)]

    def rest(dy, n):
        hi, lo = ys(dy)
        return wb.at[hi, lo, c, n]

    barrier = pltpu.get_barrier_semaphore()
    partners = [at(dx=1), at(dx=-1), at(dy=1), at(dy=-1), at(dy=2), at(dz=1), at(dz=-1), at(other=True)]
    peers = [(peer(step) * 2 + c, fsdp) for step in range(1, CHIPS)]
    for partner in partners + peers:
        pl.semaphore_signal(barrier, inc=1, device_id=partner, device_id_type=MESH)
    local = []
    for n, (ref, dst) in enumerate([
        (wkv_ref, kv_rows),
        (wq_ref, wa.at[y_hi, y_lo, c, 0]),
        (hidden_hbm, hidden_ref), (gain_hbm, gain_ref),
        (cos_hbm.at[:, y_hi], cos_ref), (sin_hbm.at[:, y_hi], sin_ref), (cart_hbm, cart_ref), (g_hbm, g_ref),
    ]):
        copy = pltpu.make_async_copy(ref, dst, local_sem.at[n])
        copy.start()
        local.append(copy)
    local[0].wait()
    kv_wide[...] = kv_rows[...].astype(F32)
    for i in range(2):
        wb[y_hi, y_lo, c, 0, :, i * HD:(i + 1) * HD] = kv_wide[pl.ds(i, 128, 2)].astype(BF16)
    pl.semaphore_wait(barrier, len(partners) + len(peers))

    def main_from_z(i):
        if i == 4:
            arrived(("za", 4, 1))
            arrived(("za", 4, -1))
        for way in (1, -1):
            if 0 < i < 4:
                arrived(("za", way * i))
            if i < 3:
                ref = main(0, SLOT[way * i]).at[0] if i else wq_ref
                send(("za", way * (i + 1)), ref, at(dz=-way), main(0, SLOT[way * (i + 1)]).at[0])
        if i == 3:
            for way, part in ((1, pl.ds(0, 64)), (-1, pl.ds(64, MAIN - 64))):
                send(("za", 4, way), main(0, SLOT[3 * way]).at[:, part], at(dz=-way), main(0, SLOT[4]).at[:, part])
        n, count = TICKS[i]
        for slot in range(n, n + count):
            for way in (1, -1):
                ref = main(0, slot).at[0]
                send(("ya", -way, slot), ref if i else wq_ref, at(dy=way), ref)

    def main_from_y(i):
        n, count = TICKS[i]
        for way in (1, -1):
            slot = n + (1 - way) // 2 if count == 2 else n
            arrived(("ya", way, slot))
            ref = main(way, slot)
            if count == 1:
                ref = ref.at[:, pl.ds(0, 64) if way == 1 else pl.ds(64, MAIN - 64)]
            send(("ya", 2, way, i), ref, at(dy=-way))
        if count == 2:
            arrived(("ya", 1, n + 1))
            arrived(("ya", -1, n))

    def main_to_core(i):
        n, count = TICKS[i]
        arrived(("ya", 2, 1, i))
        arrived(("ya", 2, -1, i))
        send(("ca", i), wa.at[:, :, c, pl.ds(n, count)], at(other=True))

    def rest_along_y():
        for way in (1, -1):
            send(("yb", -way), rest(0, 0), at(dy=way))

    def rest_further_along_y():
        for way in (1, -1):
            arrived(("yb", way))
            send(("yb", 2, way), rest(way, 0).at[pl.ds(0 if way == 1 else 64, 64)], at(dy=-way))

    def rest_from_z(i):
        if i == 0:
            arrived(("yb", 2, 1))
            arrived(("yb", 2, -1))
        for hi in range(2):
            if i == 4:
                arrived(("zb", 4, hi))
                continue
            for way in (1, -1):
                here = wb.at[hi, :, c, SLOT[way * i]]
                if i:
                    arrived(("zb", way * i, hi))
                if i < 3:
                    send(("zb", way * (i + 1), hi), here, at(dz=-way), wb.at[hi, :, c, SLOT[way * (i + 1)]])
                elif way == 1 - 2 * hi:
                    send(("zb", 4, hi), here, at(dz=-way), wb.at[hi, :, c, SLOT[4]])
        n, count = TICKS[i]
        send(("cb", i), wb.at[:, :, c, pl.ds(n, count)], at(other=True))

    def rows_out(part):
        n, count = X_PARTS[part]
        for way in (1, -1):
            send(("x", -way, part), xn.at[x, pl.ds(n, count)], at(dx=way))

    def rows_on(part):
        n, count = X_PARTS[part]
        for way in (1, -1):
            arrived(("x", way, part))
            send(("x", 2, way, part), xn.at[xs(way), pl.ds(n, count), (1 - way) // 2], at(dx=-way))

    def rows_ready(part):
        arrived(("x", 2, 1, part))
        arrived(("x", 2, -1, part))

    def operands(weights, n, hi):
        left = jnp.concatenate([xn[:, n, lo].reshape(512, 256) for lo in range(2)], axis=1)
        right = [weights[hi, lo, core, n] for lo in range(2) for core in range(2)]
        return left, jnp.concatenate(right, axis=0)

    def multiply_kv(n, hi):
        term = jnp.dot(*operands(wb, n, hi), preferred_element_type=F32)
        acc_kv[hi] = acc_kv[hi] + term if n else term

    def multiply_q(n, hi):
        term = jnp.dot(*operands(wa, n, hi), preferred_element_type=F32)
        acc_q[hi] = acc_q[hi] + term if n else term

    def multiply_all(i):
        arrived(("ca", i))
        arrived(("cb", i))
        n, count = TICKS[i]
        for slot in range(n, n + count):
            for hi in range(2):
                multiply_kv(slot, hi)
                multiply_q(slot, hi)

    rest_along_y()
    main_from_z(0)
    local[1].wait()
    local[2].wait()
    local[3].wait()
    hidden = hidden_ref[...].astype(F32)
    inverse = lax.rsqrt(jnp.mean(hidden * hidden, axis=-1, keepdims=True) + EPS)
    for n, step in enumerate(STEPS):
        for lo in range(2):
            k = lo * 8 + lax.rem(z + step + 8, 8)
            cols = pl.ds(pl.multiple_of(k * 256, 256), 256)
            part = hidden_ref[:, cols].astype(F32) * inverse * gain_ref[:, cols]
            xn[x, n, lo] = part.astype(BF16)
    rows_out(0)
    rows_out(1)
    for copy in local[4:]:
        copy.wait()
    vt_cart[:HD] = cart_ref[1].astype(F32).T.astype(BF16)
    vt_cart[HD:] = jnp.ones((vt_cart.shape[0] - HD, cart), BF16)
    grad[...] = jnp.zeros_like(grad)
    rest_further_along_y()
    main_from_z(1)
    rest_from_z(0)
    main_from_y(0)
    main_from_z(2)
    rest_from_z(1)
    main_from_y(1)
    main_to_core(0)
    main_from_z(3)
    rows_on(0)
    rows_out(2)
    rest_from_z(2)
    main_from_y(2)
    main_to_core(1)
    main_from_z(4)
    rows_ready(0)
    multiply_all(0)
    rest_from_z(3)
    main_from_y(3)
    main_to_core(2)
    rows_on(1)
    multiply_all(1)
    main_from_y(4)
    main_to_core(3)
    rest_from_z(4)
    rows_on(2)
    rows_ready(1)
    multiply_all(2)
    theirs = 1 - y_hi

    cos, sin = cos_ref[...].reshape(512, HD), sin_ref[...].reshape(512, HD)

    def turned(part):
        return (part * cos + pltpu.roll(part, HD // 2, 1) * sin).astype(BF16).reshape(4, HD, HD)

    def finish_kv(hi, out):
        out[0] = turned(acc_kv[hi, :, :HD])
        out[1] = acc_kv[hi, :, HD:].astype(BF16).reshape(4, HD, HD)

    def spots(hi, index):
        return (index // HD) * (2 * HD) + hi * HD + lax.rem(index, HD)

    def take_keys(hi, blocks):
        spare = jnp.broadcast_to(cart_ref[0, 0:1, :], (HD, HD))
        for n in range(4):
            live = spots(hi, n * HD + lax.broadcasted_iota(jnp.int32, (HD, HD), 0)) < length
            k_new[hi, n * HD:(n + 1) * HD] = jnp.where(live, blocks[0, n], spare)
            values = jnp.where(live, blocks[1, n].astype(F32), 0.0)
            vt_new[hi, :HD, n * HD:(n + 1) * HD] = values.T.astype(BF16)
        live = spots(hi, lax.broadcasted_iota(jnp.int32, (vt_new.shape[1] - HD, 4 * HD), 1)) < length
        vt_new[hi, HD:] = jnp.where(live, 1.0, 0.0).astype(BF16)

    rows_ready(2)
    arrived(("cb", 3))
    arrived(("cb", 4))
    for n in (5, 6, 7):
        multiply_kv(n, theirs)
    first_kv = len(started)
    finish_kv(theirs, kv_out)
    send("kv", kv_out, at(dy=2), kv_in)
    main_to_core(4)
    for n in (5, 6, 7):
        multiply_kv(n, y_hi)
    finish_kv(y_hi, kv_own)
    take_keys(y_hi, kv_own)
    arrived(("ca", 3))
    for n in (5, 6):
        for hi in (0, 1):
            multiply_q(n, hi)
    arrived(("ca", 4))
    multiply_q(7, theirs)
    first_q = len(started)
    for head in range(4):
        q_out[head] = turned(acc_q[theirs, :, head * HD:(head + 1) * HD])
        if head < 3:
            send(("q", head), q_out.at[head], at(dy=2), q_in.at[head])
    for j in (1, 0):
        blocks = pl.ds(2 * j, 2)
        send(("q", 3, j), q_out.at[3, blocks], at(dy=2), q_in.at[3, blocks])
    multiply_q(7, y_hi)
    for head in range(4):
        q_own[head] = turned(acc_q[y_hi, :, head * HD:(head + 1) * HD])

    def grad_rows(head, j, hi):
        columns = pl.ds(pl.multiple_of(head * HD, HD), HD)
        g = g_ref[2 * j:2 * j + 2, hi, :, columns].reshape(2 * HD, HD)
        row = lax.broadcasted_iota(jnp.int32, (2 * HD, HD), 0)
        row = 4 * j * HD + (row // HD) * (2 * HD) + hi * HD + lax.rem(row, HD)
        return jnp.where(row < length, g, jnp.zeros_like(g))

    def new_scores(key_hi, hi, j, q):
        near = lax.dot_general(k_new[key_hi, 2 * j * HD:2 * (j + 1) * HD], q, NT, preferred_element_type=F32)
        key = spots(key_hi, lax.broadcasted_iota(jnp.int32, near.shape, 0))
        row = spots(hi, lax.broadcasted_iota(jnp.int32, (1, 2 * HD), 1))
        near = jnp.where(key <= row, near, -jnp.inf)
        if j == 0:
            return [near]
        return [lax.dot_general(k_new[key_hi, :2 * j * HD], q, NT, preferred_element_type=F32), near]

    def highest(tops, scores):
        for part in scores:
            tops = jnp.maximum(tops, jnp.max(part, axis=0, keepdims=True))
        return tops

    def add_values(out, key_hi, scores, top):
        first = 0
        for part in scores:
            last = first + part.shape[0]
            weights = jnp.exp2((part - top) * factor).astype(BF16)
            out += jnp.dot(vt_new[key_hi, :, first:last], weights, preferred_element_type=F32)
            first = last
        return out

    def first_part(key_hi, hi, js, qs, gs):
        carts = [lax.dot_general(cart_ref[0], q, NT, preferred_element_type=F32) for q in qs]
        news = [new_scores(key_hi, hi, j, q) for j, q in zip(js, qs)]
        d_probs = [lax.dot_general(cart_ref[1], g, NT, preferred_element_type=F32) for g in gs]
        kept = []
        for scores, new, d_prob in zip(carts, news, d_probs):
            top = highest(jnp.max(scores, axis=0, keepdims=True), new)
            e_cart = jnp.exp2((scores - top) * factor)
            out = jnp.dot(vt_cart[...], e_cart.astype(BF16), preferred_element_type=F32)
            kept.append((e_cart, top, d_prob, add_values(out, key_hi, new, top)))
        return kept

    def second_part(head, key_hi, hi, js, qs, gs, kept):
        columns = pl.ds(pl.multiple_of(head * HD, HD), HD)
        news = [new_scores(key_hi, hi, j, q) for j, q in zip(js, qs)]
        outs = []
        for new, (_, before, _, out) in zip(news, kept):
            top = highest(before, new)
            shrink = jnp.exp2((before - top) * factor)
            outs.append((add_values(out * shrink, key_hi, new, top), shrink))
        probs, scores = [], []
        for j, g, (out, shrink), (e_cart, _, d_prob, _) in zip(js, gs, outs, kept):
            inverse = 1.0 / out[HD:HD + 1]
            out = out[:HD] * inverse
            mixed_ref[2 * j:2 * j + 2, hi, :, columns] = out.T.astype(BF16).reshape(2, HD, HD)
            delta = jnp.sum(out * g.astype(F32).T, axis=0, keepdims=True)
            prob = e_cart * (shrink * inverse)
            scores.append((prob * (d_prob - delta)).astype(BF16))
            probs.append(prob.astype(BF16))
        join = functools.partial(jnp.concatenate, axis=0)
        grad[1] += jnp.dot(jnp.concatenate(probs, axis=1), join(gs), preferred_element_type=F32)
        grad[0] += jnp.dot(jnp.concatenate(scores, axis=1), join(qs), preferred_element_type=F32)

    def pairs(q_ref, head, hi, js=(0, 1)):
        qs = [q_ref[head, 2 * j:2 * j + 2].reshape(2 * HD, HD) for j in js]
        return qs, [grad_rows(head, j, hi) for j in js]

    both = (0, 1)

    @pl.loop(0, 4)
    def _(head):
        for j, kept in enumerate(first_part(y_hi, y_hi, both, *pairs(q_own, head, y_hi))):
            e_keep[head, j], top_keep[head, j], d_keep[head, j], out_keep[head, j] = kept

    for copy in started[:first_kv]:
        copy.wait_send()
    arrived("kv")
    take_keys(theirs, kv_in)

    @pl.loop(0, 4)
    def _(head):
        kept = [(e_keep[head, j], top_keep[head, j], d_keep[head, j], out_keep[head, j]) for j in both]
        second_part(head, theirs, y_hi, both, *pairs(q_own, head, y_hi), kept)

    @pl.loop(0, 3)
    def _(head):
        pltpu.make_async_remote_copy(
            src_ref=q_out.at[head], dst_ref=q_in.at[head], send_sem=send_sem.at[first_q + head],
            recv_sem=recv_sem.at[first_q + head], device_id=at(dy=2), device_id_type=MESH,
        ).wait_recv()
        qs, gs = pairs(q_in, head, theirs)
        second_part(head, theirs, theirs, both, qs, gs, first_part(y_hi, theirs, both, qs, gs))

    for j in (1, 0):
        arrived(("q", 3, j))
        qs, gs = pairs(q_in, 3, theirs, (j,))
        second_part(3, theirs, theirs, (j,), qs, gs, first_part(y_hi, theirs, (j,), qs, gs))

    rows = cart
    send("core_sum", grad.at[1 - c], at(other=True), from_core)
    arrived("core_sum")
    half[...] = (grad[c] + from_core[...]).reshape(half.shape)
    to_chips[...] = half[...].astype(BF16)
    for step in FAR_FIRST:
        send(("rs", step), to_chips.at[peer(step)], peers[step - 1], from_chips.at[step])
    done = len(started)
    for copy in started[first_kv:]:
        copy.wait_send()
    total = half[chip]
    for step in reversed(FAR_FIRST):
        arrived(("rs", step))
        total += from_chips[step].astype(F32)
    total = total * jnp.where(c == 0, scale, 1.0)
    gathered[chip] = total.astype(BF16)
    for step in FAR_FIRST:
        send(("ag", step), gathered.at[chip], peers[step - 1])
    for step in range(1, CHIPS):
        arrived(("ag", step))
    send("core_back", gathered, at(other=True), other)
    sum_ref[c] = gathered[...].reshape(rows, HD)
    arrived("core_back")
    sum_ref[1 - c] = other[...].reshape(rows, HD)
    for copy in started[done:]:
        copy.wait_send()


def rope_tables(cart, seq):
    frequency = np.power(np.float32(ROPE_BASE), np.arange(HD // 2, dtype=np.float32) * np.float32(-2.0 / HD))
    angles = (cart + np.arange(seq, dtype=np.float32))[:, None] * frequency.astype(np.float32)[None, :]
    cos, sin = np.cos(angles), np.sin(angles)
    shape = (seq // 256, 2, 128, HD)
    return (
        np.concatenate([cos, cos], axis=1).astype(np.float32).reshape(shape),
        np.concatenate([-sin, sin], axis=1).astype(np.float32).reshape(shape),
    )


def tail_kernel(mixed_ref, sum_ref, mixed_out, sum_out):
    mixed_out[...] = mixed_ref[...]
    sum_out[...] = sum_ref[...].astype(F32)


def on_device(hidden_in, lengths, cartridge, norm_gain, w_query, w_keyval, cotangent):
    cart = cartridge.shape[1]
    vmem, hbm = pl.BlockSpec(memory_space=pltpu.VMEM), pl.BlockSpec(memory_space=pltpu.HBM)
    cos, sin = rope_tables(cart, 1024)
    copies, share = 120, cart // CHIPS
    mixed, summed = pl.pallas_call(
        layer_kernel,
        name="layer",
        out_shape=(
            jax.ShapeDtypeStruct((4, 2, 128, 512), BF16),
            jax.ShapeDtypeStruct((2, cart, HD), BF16),
        ),
        in_specs=[pl.BlockSpec(memory_space=pltpu.SMEM)] + [hbm] * 8,
        out_specs=(vmem,) * 2,
        scratch_shapes=[
            pltpu.VMEM((128, 4096), BF16),
            pltpu.VMEM((1, 4096), F32),
            pltpu.VMEM((4, 128, HD), F32),
            pltpu.VMEM((4, 128, HD), F32),
            pltpu.VMEM((2, cart, HD), BF16),
            pltpu.VMEM((4, 2, 128, 512), BF16),
            pltpu.VMEM((4, 8, 2, 128, 256), BF16),
            pltpu.VMEM((2, 2, 2, 8, MAIN, 512), BF16),
            pltpu.VMEM((2, 2, 2, 8, 128, 256), BF16),
            pltpu.VMEM((2, 512, 512), F32),
            pltpu.VMEM((2, 512, 256), F32),
            pltpu.VMEM((4, 4, 128, HD), BF16),
            pltpu.VMEM((2, 4, 128, HD), BF16),
            pltpu.VMEM((4, 4, 128, HD), BF16),
            pltpu.VMEM((2, 4, 128, HD), BF16),
            pltpu.VMEM((4, 4, 128, HD), BF16),
            pltpu.VMEM((2, 4, 128, HD), BF16),
            pltpu.VMEM((2, 512, HD), BF16),
            pltpu.VMEM((HD + 16, cart), BF16),
            pltpu.VMEM((2, HD + 16, 512), BF16),
            pltpu.VMEM((4, 2, cart, 256), F32),
            pltpu.VMEM((4, 2, cart, 256), F32),
            pltpu.VMEM((4, 2, 1, 256), F32),
            pltpu.VMEM((4, 2, HD + 16, 256), F32),
            pltpu.VMEM((2, cart, HD), F32),
            pltpu.VMEM((cart, HD), F32),
            pltpu.VMEM((CHIPS, share, HD), F32),
            pltpu.VMEM((CHIPS, share, HD), BF16),
            pltpu.VMEM((CHIPS, share, HD), BF16),
            pltpu.VMEM((CHIPS, share, HD), BF16),
            pltpu.VMEM((CHIPS, share, HD), BF16),
            pltpu.VMEM((256, HD), BF16),
            pltpu.VMEM((256, HD), F32),
            pltpu.SemaphoreType.DMA((8,)),
            pltpu.SemaphoreType.DMA((copies,)),
            pltpu.SemaphoreType.DMA((copies,)),
        ],
        compiler_params=pltpu.CompilerParams(collective_id=0, has_side_effects=True, vmem_limit_bytes=60 << 20),
    )(lengths, hidden_in, norm_gain.reshape(1, -1), w_query, w_keyval.reshape(256, HD), cos, sin, cartridge,
      cotangent.reshape(4, 2, 128, 512))
    blocks = (
        pl.BlockSpec((2, 2, 128, 512), lambda i: (i, 0, 0, 0)),
        pl.BlockSpec((1, cart, HD), lambda i: (i, 0, 0)),
    )
    mixed, summed = pl.pallas_call(
        tail_kernel,
        name="tail",
        out_shape=(
            jax.ShapeDtypeStruct(mixed.shape, BF16),
            jax.ShapeDtypeStruct(summed.shape, F32),
        ),
        grid=(2,),
        in_specs=blocks,
        out_specs=blocks,
    )(mixed, summed)
    return mixed.reshape(1024, 512), summed


def solution(mesh):
    in_specs = (
        P(("dp", "fsdp"), None),
        P("dp"),
        P(None, None, "fsdp"),
        P(),
        P("dp", "fsdp"),
        P("dp", None, "fsdp"),
        P("dp", "fsdp"),
    )
    out_specs = (P("dp", "fsdp"), P(None, None, "fsdp"))
    return jax.shard_map(on_device, mesh=mesh, in_specs=in_specs, out_specs=out_specs, check_vma=False)
```

```python
import functools
import math

import jax
import jax.numpy as jnp
import numpy as np
from jax import lax
from jax.experimental import pallas as pl
from jax.experimental.pallas import tpu as pltpu
from jax.sharding import PartitionSpec as P

HD = 128
MESH = pl.DeviceIdType.MESH
EPS = 1e-05
ROPE_BASE = 500000.0
F32 = jnp.float32
BF16 = jnp.bfloat16
NT = (((1,), (1,)), ((), ()))
CHIPS = 16
FAR_FIRST = sorted(range(1, CHIPS), key=lambda step: -min(step % 8, 8 - step % 8))
STEPS = (0, 1, -1, 2, -2, 3, -3, 4)
SLOT = {step: n for n, step in enumerate(STEPS)}
TICKS = ((0, 1), (1, 2), (3, 2), (5, 2), (7, 1))
X_PARTS = ((0, 3), (3, 2), (5, 3))
MAIN = 128

def layer_kernel(len_ref, hidden_hbm, gain_hbm, wq_ref, wkv_ref, cos_hbm, sin_hbm, cart_hbm, g_hbm,
                 mixed_ref, sum_ref,
                 hidden_ref, gain_ref, cos_ref, sin_ref, cart_ref, g_ref,
                 xn, wa, wb, acc_q, acc_kv, q_out, kv_out, q_in, kv_in, q_own, kv_own,
                 k_new, vt_cart, vt_new, e_keep, d_keep, g_turned, top_keep, out_keep, grad, from_core, half, to_chips, from_chips, gathered, other,
                 kv_rows, kv_wide, local_sem, send_sem, recv_sem):
    dp, fsdp = lax.axis_index("dp"), lax.axis_index("fsdp")
    x, y_hi, y_lo, z, c = fsdp // 2, fsdp % 2, dp // 16, (dp // 2) % 8, dp % 2
    chip = dp // 2
    y = y_hi * 2 + y_lo
    turn = 1 - 2 * c
    length = len_ref[0]
    cart, seq = cart_ref.shape[1], 1024
    scale = HD ** -0.5
    factor = scale * math.log2(math.e)

    def at(dx=0, dy=0, dz=0, other=False):
        yy = lax.rem(y + dy + 8, 4)
        return (
            lax.rem(yy, 2) * 16 + lax.rem(z + dz + 16, 8) * 2 + (1 - c if other else c),
            lax.rem(x + dx + 8, 4) * 2 + yy // 2,
        )

    def peer(step):
        return lax.rem(chip + step, CHIPS)

    def ys(dy):
        yy = lax.rem(y + dy + 8, 4)
        return yy // 2, lax.rem(yy, 2)

    def xs(dx):
        return lax.rem(x + dx + 8, 4)

    slots, started = {}, []

    def send(name, ref, target, dst=None):
        assert name not in slots
        copy = pltpu.make_async_remote_copy(
            src_ref=ref, dst_ref=ref if dst is None else dst,
            send_sem=send_sem.at[len(started)], recv_sem=recv_sem.at[len(started)],
            device_id=target, device_id_type=MESH,
        )
        copy.start()
        slots[name] = copy
        started.append(copy)

    def arrived(name):
        slots[name].wait_recv()

    def main(dy, n, count=1):
        hi, lo = ys(dy)
        return wa.at[hi, lo, c, pl.ds(n, count)]

    def rest(dy, n):
        hi, lo = ys(dy)
        return wb.at[hi, lo, c, n]

    barrier = pltpu.get_barrier_semaphore()
    partners = [at(dx=1), at(dx=-1), at(dy=1), at(dy=-1), at(dy=2), at(dz=1), at(dz=-1), at(other=True)]
    peers = [(peer(step) * 2 + c, fsdp) for step in range(1, CHIPS)]
    for partner in partners + peers:
        pl.semaphore_signal(barrier, inc=1, device_id=partner, device_id_type=MESH)
    local = []
    for n, (ref, dst) in enumerate([
        (wkv_ref, kv_rows),
        (wq_ref, wa.at[y_hi, y_lo, c, 0]),
        (hidden_hbm, hidden_ref), (gain_hbm, gain_ref),
        (cos_hbm.at[:, y_hi], cos_ref), (sin_hbm.at[:, y_hi], sin_ref), (cart_hbm, cart_ref), (g_hbm, g_ref),
    ]):
        copy = pltpu.make_async_copy(ref, dst, local_sem.at[n])
        copy.start()
        local.append(copy)
    local[0].wait()
    kv_wide[...] = kv_rows[...].astype(F32)
    for i in range(2):
        wb[y_hi, y_lo, c, 0, :, i * HD:(i + 1) * HD] = kv_wide[pl.ds(i, 128, 2)].astype(BF16)
    pl.semaphore_wait(barrier, len(partners) + len(peers))

    def main_from_z(i):
        if i == 4:
            arrived(("za", 4, 1))
            arrived(("za", 4, -1))
        for way in (1, -1):
            if 0 < i < 4:
                arrived(("za", way * i))
            if i < 3:
                ref = main(0, SLOT[way * i]).at[0] if i else wq_ref
                send(("za", way * (i + 1)), ref, at(dz=-way), main(0, SLOT[way * (i + 1)]).at[0])
        if i == 3:
            for way, part in ((1, pl.ds(0, 64)), (-1, pl.ds(64, MAIN - 64))):
                send(("za", 4, way), main(0, SLOT[3 * way]).at[:, part], at(dz=-way), main(0, SLOT[4]).at[:, part])
        n, count = TICKS[i]
        for slot in range(n, n + count):
            for way in (1, -1):
                ref = main(0, slot).at[0]
                send(("ya", -way, slot), ref if i else wq_ref, at(dy=way), ref)

    def main_from_y(i):
        n, count = TICKS[i]
        for way in (1, -1):
            slot = n + (1 - way) // 2 if count == 2 else n
            arrived(("ya", way, slot))
            ref = main(way, slot)
            if count == 1:
                ref = ref.at[:, pl.ds(0, 64) if way == 1 else pl.ds(64, MAIN - 64)]
            send(("ya", 2, way, i), ref, at(dy=-way))
        if count == 2:
            arrived(("ya", 1, n + 1))
            arrived(("ya", -1, n))

    def main_to_core(i):
        n, count = TICKS[i]
        arrived(("ya", 2, 1, i))
        arrived(("ya", 2, -1, i))
        send(("ca", i), wa.at[:, :, c, pl.ds(n, count)], at(other=True))

    def rest_along_y():
        for way in (1, -1):
            send(("yb", -way), rest(0, 0), at(dy=way))

    def rest_further_along_y():
        for way in (1, -1):
            arrived(("yb", way))
            send(("yb", 2, way), rest(way, 0).at[pl.ds(0 if way == 1 else 64, 64)], at(dy=-way))

    def rest_from_z(i):
        if i == 0:
            arrived(("yb", 2, 1))
            arrived(("yb", 2, -1))
        for hi in range(2):
            if i == 4:
                arrived(("zb", 4, hi))
                continue
            for way in (1, -1):
                here = wb.at[hi, :, c, SLOT[way * i]]
                if i:
                    arrived(("zb", way * i, hi))
                if i < 3:
                    send(("zb", way * (i + 1), hi), here, at(dz=-way), wb.at[hi, :, c, SLOT[way * (i + 1)]])
                elif way == 1 - 2 * hi:
                    send(("zb", 4, hi), here, at(dz=-way), wb.at[hi, :, c, SLOT[4]])
        n, count = TICKS[i]
        send(("cb", i), wb.at[:, :, c, pl.ds(n, count)], at(other=True))

    def rows_out(part):
        n, count = X_PARTS[part]
        for way in (1, -1):
            send(("x", -way, part), xn.at[x, pl.ds(n, count)], at(dx=way))

    def rows_on(part):
        n, count = X_PARTS[part]
        for way in (1, -1):
            arrived(("x", way, part))
            send(("x", 2, way, part), xn.at[xs(way), pl.ds(n, count), (1 - way) // 2], at(dx=-way))

    def rows_ready(part):
        arrived(("x", 2, 1, part))
        arrived(("x", 2, -1, part))

    def operands(weights, n, hi):
        left = jnp.concatenate([xn[:, n, lo].reshape(512, 256) for lo in range(2)], axis=1)
        right = [weights[hi, lo, core, n] for lo in range(2) for core in range(2)]
        return left, jnp.concatenate(right, axis=0)

    def multiply_kv(n, hi):
        term = jnp.dot(*operands(wb, n, hi), preferred_element_type=F32)
        acc_kv[hi] = acc_kv[hi] + term if n else term

    def multiply_q(n, hi):
        term = jnp.dot(*operands(wa, n, hi), preferred_element_type=F32)
        acc_q[hi] = acc_q[hi] + term if n else term

    def multiply_all(i):
        arrived(("ca", i))
        arrived(("cb", i))
        n, count = TICKS[i]
        for slot in range(n, n + count):
            for hi in range(2):
                multiply_kv(slot, hi)
                multiply_q(slot, hi)

    rest_along_y()
    main_from_z(0)
    local[1].wait()
    local[2].wait()
    local[3].wait()
    hidden = hidden_ref[...].astype(F32)
    inverse = lax.rsqrt(jnp.mean(hidden * hidden, axis=-1, keepdims=True) + EPS)
    for n, step in enumerate(STEPS):
        for lo in range(2):
            k = lo * 8 + lax.rem(z + step + 8, 8)
            cols = pl.ds(pl.multiple_of(k * 256, 256), 256)
            part = hidden_ref[:, cols].astype(F32) * inverse * gain_ref[:, cols]
            xn[x, n, lo] = part.astype(BF16)
    rows_out(0)
    rows_out(1)
    for copy in local[4:]:
        copy.wait()
    vt_cart[:HD] = cart_ref[1].astype(F32).T.astype(BF16)
    vt_cart[HD:] = jnp.ones((vt_cart.shape[0] - HD, cart), BF16)
    grad[...] = jnp.zeros_like(grad)
    def grad_rows(head, j, hi):
        columns = pl.ds(pl.multiple_of(head * HD, HD), HD)
        g = g_ref[2 * j:2 * j + 2, hi, :, columns].reshape(2 * HD, HD)
        row = lax.broadcasted_iota(jnp.int32, (2 * HD, HD), 0)
        row = 4 * j * HD + (row // HD) * (2 * HD) + hi * HD + lax.rem(row, HD)
        return jnp.where(row < length, g, jnp.zeros_like(g))

    def value_products(hi):
        @pl.loop(0, 4)
        def _(head):
            for j in range(2):
                g = grad_rows(head, j, hi)
                d_keep[hi, head, j] = lax.dot_general(cart_ref[1], g, NT, preferred_element_type=F32)
                g_turned[hi, head, j] = g.astype(F32).T

    value_products(y_hi)
    rest_further_along_y()
    main_from_z(1)
    rest_from_z(0)
    main_from_y(0)
    main_from_z(2)
    rest_from_z(1)
    main_from_y(1)
    main_to_core(0)
    main_from_z(3)
    rows_on(0)
    rows_out(2)
    rest_from_z(2)
    main_from_y(2)
    main_to_core(1)
    main_from_z(4)
    value_products(1 - y_hi)
    rows_ready(0)
    multiply_all(0)
    rest_from_z(3)
    main_from_y(3)
    main_to_core(2)
    rows_on(1)
    multiply_all(1)
    main_from_y(4)
    main_to_core(3)
    rest_from_z(4)
    rows_on(2)
    rows_ready(1)
    multiply_all(2)
    theirs = 1 - y_hi

    cos, sin = cos_ref[...].reshape(512, HD), sin_ref[...].reshape(512, HD)

    def turned(part):
        return (part * cos + pltpu.roll(part, HD // 2, 1) * sin).astype(BF16).reshape(4, HD, HD)

    def finish_kv(hi, out):
        out[0] = turned(acc_kv[hi, :, :HD])
        out[1] = acc_kv[hi, :, HD:].astype(BF16).reshape(4, HD, HD)

    def spots(hi, index):
        return (index // HD) * (2 * HD) + hi * HD + lax.rem(index, HD)

    def take_keys(hi, blocks):
        spare = jnp.broadcast_to(cart_ref[0, 0:1, :], (HD, HD))
        for n in range(4):
            live = spots(hi, n * HD + lax.broadcasted_iota(jnp.int32, (HD, HD), 0)) < length
            k_new[hi, n * HD:(n + 1) * HD] = jnp.where(live, blocks[0, n], spare)
            values = jnp.where(live, blocks[1, n].astype(F32), 0.0)
            vt_new[hi, :HD, n * HD:(n + 1) * HD] = values.T.astype(BF16)
        live = spots(hi, lax.broadcasted_iota(jnp.int32, (vt_new.shape[1] - HD, 4 * HD), 1)) < length
        vt_new[hi, HD:] = jnp.where(live, 1.0, 0.0).astype(BF16)

    rows_ready(2)
    arrived(("cb", 3))
    arrived(("cb", 4))
    for n in (5, 6, 7):
        multiply_kv(n, theirs)
    first_kv = len(started)
    finish_kv(theirs, kv_out)
    send("kv", kv_out, at(dy=2), kv_in)
    main_to_core(4)
    for n in (5, 6, 7):
        multiply_kv(n, y_hi)
    finish_kv(y_hi, kv_own)
    take_keys(y_hi, kv_own)
    arrived(("ca", 3))
    for n in (5, 6):
        for hi in (0, 1):
            multiply_q(n, hi)
    arrived(("ca", 4))
    multiply_q(7, theirs)
    first_q = len(started)
    for head in range(4):
        q_out[head] = turned(acc_q[theirs, :, head * HD:(head + 1) * HD])
        if head < 3:
            send(("q", head), q_out.at[head], at(dy=2), q_in.at[head])
    for j in (1, 0):
        blocks = pl.ds(2 * j, 2)
        send(("q", 3, j), q_out.at[3, blocks], at(dy=2), q_in.at[3, blocks])
    multiply_q(7, y_hi)
    for head in range(4):
        q_own[head] = turned(acc_q[y_hi, :, head * HD:(head + 1) * HD])

    def new_scores(key_hi, hi, j, q):
        near = lax.dot_general(k_new[key_hi, 2 * j * HD:2 * (j + 1) * HD], q, NT, preferred_element_type=F32)
        key = spots(key_hi, lax.broadcasted_iota(jnp.int32, near.shape, 0))
        row = spots(hi, lax.broadcasted_iota(jnp.int32, (1, 2 * HD), 1))
        near = jnp.where(key <= row, near, -jnp.inf)
        if j == 0:
            return [near]
        return [lax.dot_general(k_new[key_hi, :2 * j * HD], q, NT, preferred_element_type=F32), near]

    def highest(tops, scores):
        for part in scores:
            tops = jnp.maximum(tops, jnp.max(part, axis=0, keepdims=True))
        return tops

    def add_values(out, key_hi, scores, top):
        first = 0
        for part in scores:
            last = first + part.shape[0]
            weights = jnp.exp2((part - top) * factor).astype(BF16)
            out += jnp.dot(vt_new[key_hi, :, first:last], weights, preferred_element_type=F32)
            first = last
        return out

    def first_part(key_hi, hi, js, qs):
        carts = [lax.dot_general(cart_ref[0], q, NT, preferred_element_type=F32) for q in qs]
        news = [new_scores(key_hi, hi, j, q) for j, q in zip(js, qs)]
        kept = []
        for scores, new in zip(carts, news):
            top = highest(jnp.max(scores, axis=0, keepdims=True), new)
            e_cart = jnp.exp2((scores - top) * factor)
            out = jnp.dot(vt_cart[...], e_cart.astype(BF16), preferred_element_type=F32)
            kept.append((e_cart, top, add_values(out, key_hi, new, top)))
        return kept

    def second_part(head, key_hi, hi, js, qs, gs, kept):
        columns = pl.ds(pl.multiple_of(head * HD, HD), HD)
        news = [new_scores(key_hi, hi, j, q) for j, q in zip(js, qs)]
        outs = []
        for new, (_, before, out) in zip(news, kept):
            top = highest(before, new)
            shrink = jnp.exp2((before - top) * factor)
            outs.append((add_values(out * shrink, key_hi, new, top), shrink))
        probs, scores = [], []
        for j, (out, shrink), (e_cart, _, _) in zip(js, outs, kept):
            inverse = 1.0 / out[HD:HD + 1]
            out = out[:HD] * inverse
            mixed_ref[2 * j:2 * j + 2, hi, :, columns] = out.T.astype(BF16).reshape(2, HD, HD)
            delta = jnp.sum(out * g_turned[hi, head, j], axis=0, keepdims=True)
            prob = e_cart * (shrink * inverse)
            scores.append((prob * (d_keep[hi, head, j] - delta)).astype(BF16))
            probs.append(prob.astype(BF16))
        join = functools.partial(jnp.concatenate, axis=0)
        grad[1] += jnp.dot(jnp.concatenate(probs, axis=1), join(gs), preferred_element_type=F32)
        grad[0] += jnp.dot(jnp.concatenate(scores, axis=1), join(qs), preferred_element_type=F32)

    def pairs(q_ref, head, hi, js=(0, 1)):
        qs = [q_ref[head, 2 * j:2 * j + 2].reshape(2 * HD, HD) for j in js]
        return qs, [grad_rows(head, j, hi) for j in js]

    both = (0, 1)

    @pl.loop(0, 4)
    def _(head):
        qs, _ = pairs(q_own, head, y_hi)
        for j, kept in enumerate(first_part(y_hi, y_hi, both, qs)):
            e_keep[head, j], top_keep[head, j], out_keep[head, j] = kept

    for copy in started[:first_kv]:
        copy.wait_send()
    arrived("kv")
    take_keys(theirs, kv_in)

    @pl.loop(0, 4)
    def _(head):
        kept = [(e_keep[head, j], top_keep[head, j], out_keep[head, j]) for j in both]
        second_part(head, theirs, y_hi, both, *pairs(q_own, head, y_hi), kept)

    @pl.loop(0, 3)
    def _(head):
        pltpu.make_async_remote_copy(
            src_ref=q_out.at[head], dst_ref=q_in.at[head], send_sem=send_sem.at[first_q + head],
            recv_sem=recv_sem.at[first_q + head], device_id=at(dy=2), device_id_type=MESH,
        ).wait_recv()
        qs, gs = pairs(q_in, head, theirs)
        second_part(head, theirs, theirs, both, qs, gs, first_part(y_hi, theirs, both, qs))

    for j in (1, 0):
        arrived(("q", 3, j))
        qs, gs = pairs(q_in, 3, theirs, (j,))
        second_part(3, theirs, theirs, (j,), qs, gs, first_part(y_hi, theirs, (j,), qs))

    rows = cart
    send("core_sum", grad.at[1 - c], at(other=True), from_core)
    arrived("core_sum")
    half[...] = (grad[c] + from_core[...]).reshape(half.shape)
    to_chips[...] = half[...].astype(BF16)
    for step in FAR_FIRST:
        send(("rs", step), to_chips.at[peer(step)], peers[step - 1], from_chips.at[step])
    done = len(started)
    for copy in started[first_kv:]:
        copy.wait_send()
    total = half[chip]
    for step in reversed(FAR_FIRST):
        arrived(("rs", step))
        total += from_chips[step].astype(F32)
    total = total * jnp.where(c == 0, scale, 1.0)
    gathered[chip] = total.astype(BF16)
    for step in FAR_FIRST:
        send(("ag", step), gathered.at[chip], peers[step - 1])
    for step in range(1, CHIPS):
        arrived(("ag", step))
    send("core_back", gathered, at(other=True), other)
    sum_ref[c] = gathered[...].reshape(rows, HD)
    arrived("core_back")
    sum_ref[1 - c] = other[...].reshape(rows, HD)
    for copy in started[done:]:
        copy.wait_send()


def rope_tables(cart, seq):
    frequency = np.power(np.float32(ROPE_BASE), np.arange(HD // 2, dtype=np.float32) * np.float32(-2.0 / HD))
    angles = (cart + np.arange(seq, dtype=np.float32))[:, None] * frequency.astype(np.float32)[None, :]
    cos, sin = np.cos(angles), np.sin(angles)
    shape = (seq // 256, 2, 128, HD)
    return (
        np.concatenate([cos, cos], axis=1).astype(np.float32).reshape(shape),
        np.concatenate([-sin, sin], axis=1).astype(np.float32).reshape(shape),
    )


def tail_kernel(mixed_ref, sum_ref, mixed_out, sum_out):
    mixed_out[...] = mixed_ref[...]
    sum_out[...] = sum_ref[...].astype(F32)


def on_device(hidden_in, lengths, cartridge, norm_gain, w_query, w_keyval, cotangent):
    cart = cartridge.shape[1]
    vmem, hbm = pl.BlockSpec(memory_space=pltpu.VMEM), pl.BlockSpec(memory_space=pltpu.HBM)
    cos, sin = rope_tables(cart, 1024)
    copies, share = 120, cart // CHIPS
    mixed, summed = pl.pallas_call(
        layer_kernel,
        name="layer",
        out_shape=(
            jax.ShapeDtypeStruct((4, 2, 128, 512), BF16),
            jax.ShapeDtypeStruct((2, cart, HD), BF16),
        ),
        in_specs=[pl.BlockSpec(memory_space=pltpu.SMEM)] + [hbm] * 8,
        out_specs=(vmem,) * 2,
        scratch_shapes=[
            pltpu.VMEM((128, 4096), BF16),
            pltpu.VMEM((1, 4096), F32),
            pltpu.VMEM((4, 128, HD), F32),
            pltpu.VMEM((4, 128, HD), F32),
            pltpu.VMEM((2, cart, HD), BF16),
            pltpu.VMEM((4, 2, 128, 512), BF16),
            pltpu.VMEM((4, 8, 2, 128, 256), BF16),
            pltpu.VMEM((2, 2, 2, 8, MAIN, 512), BF16),
            pltpu.VMEM((2, 2, 2, 8, 128, 256), BF16),
            pltpu.VMEM((2, 512, 512), F32),
            pltpu.VMEM((2, 512, 256), F32),
            pltpu.VMEM((4, 4, 128, HD), BF16),
            pltpu.VMEM((2, 4, 128, HD), BF16),
            pltpu.VMEM((4, 4, 128, HD), BF16),
            pltpu.VMEM((2, 4, 128, HD), BF16),
            pltpu.VMEM((4, 4, 128, HD), BF16),
            pltpu.VMEM((2, 4, 128, HD), BF16),
            pltpu.VMEM((2, 512, HD), BF16),
            pltpu.VMEM((HD + 16, cart), BF16),
            pltpu.VMEM((2, HD + 16, 512), BF16),
            pltpu.VMEM((4, 2, cart, 256), F32),
            pltpu.VMEM((2, 4, 2, cart, 256), F32),
            pltpu.VMEM((2, 4, 2, HD, 256), F32),
            pltpu.VMEM((4, 2, 1, 256), F32),
            pltpu.VMEM((4, 2, HD + 16, 256), F32),
            pltpu.VMEM((2, cart, HD), F32),
            pltpu.VMEM((cart, HD), F32),
            pltpu.VMEM((CHIPS, share, HD), F32),
            pltpu.VMEM((CHIPS, share, HD), BF16),
            pltpu.VMEM((CHIPS, share, HD), BF16),
            pltpu.VMEM((CHIPS, share, HD), BF16),
            pltpu.VMEM((CHIPS, share, HD), BF16),
            pltpu.VMEM((256, HD), BF16),
            pltpu.VMEM((256, HD), F32),
            pltpu.SemaphoreType.DMA((8,)),
            pltpu.SemaphoreType.DMA((copies,)),
            pltpu.SemaphoreType.DMA((copies,)),
        ],
        compiler_params=pltpu.CompilerParams(collective_id=0, has_side_effects=True, vmem_limit_bytes=60 << 20),
    )(lengths, hidden_in, norm_gain.reshape(1, -1), w_query, w_keyval.reshape(256, HD), cos, sin, cartridge,
      cotangent.reshape(4, 2, 128, 512))
    blocks = (
        pl.BlockSpec((2, 2, 128, 512), lambda i: (i, 0, 0, 0)),
        pl.BlockSpec((1, cart, HD), lambda i: (i, 0, 0)),
    )
    mixed, summed = pl.pallas_call(
        tail_kernel,
        name="tail",
        out_shape=(
            jax.ShapeDtypeStruct(mixed.shape, BF16),
            jax.ShapeDtypeStruct(summed.shape, F32),
        ),
        grid=(2,),
        in_specs=blocks,
        out_specs=blocks,
    )(mixed, summed)
    return mixed.reshape(1024, 512), summed


def solution(mesh):
    in_specs = (
        P(("dp", "fsdp"), None),
        P("dp"),
        P(None, None, "fsdp"),
        P(),
        P("dp", "fsdp"),
        P("dp", None, "fsdp"),
        P("dp", "fsdp"),
    )
    out_specs = (P("dp", "fsdp"), P(None, None, "fsdp"))
    return jax.shard_map(on_device, mesh=mesh, in_specs=in_specs, out_specs=out_specs, check_vma=False)
```

```python
import functools
import math

import jax
import jax.numpy as jnp
import numpy as np
from jax import lax
from jax.experimental import pallas as pl
from jax.experimental.pallas import tpu as pltpu
from jax.sharding import PartitionSpec as P

HD = 128
MESH = pl.DeviceIdType.MESH
EPS = 1e-05
ROPE_BASE = 500000.0
F32 = jnp.float32
BF16 = jnp.bfloat16
NT = (((1,), (1,)), ((), ()))
CHIPS = 16
FAR_FIRST = sorted(range(1, CHIPS), key=lambda step: -min(step % 8, 8 - step % 8))
STEPS = (0, 1, -1, 2, -2, 3, -3, 4)
SLOT = {step: n for n, step in enumerate(STEPS)}
TICKS = ((0, 1), (1, 2), (3, 2), (5, 2), (7, 1))
X_PARTS = ((0, 3), (3, 2), (5, 3))
MAIN = 128

def layer_kernel(len_ref, hidden_hbm, gain_hbm, wq_ref, wkv_ref, cos_hbm, sin_hbm, cart_hbm, g_hbm,
                 mixed_ref, sum_ref,
                 hidden_ref, gain_ref, cos_ref, sin_ref, cart_ref, g_ref,
                 xn, wa, wb, acc_q, acc_kv, q_out, kv_out, q_in, kv_in, q_own, kv_own,
                 k_new, vt_cart, vt_new, e_keep, d_keep, g_turned, top_keep, out_keep, grad, from_core, half, to_chips, from_chips, gathered, other,
                 kv_rows, kv_wide, local_sem, send_sem, recv_sem):
    dp, fsdp = lax.axis_index("dp"), lax.axis_index("fsdp")
    x, y_hi, y_lo, z, c = fsdp // 2, fsdp % 2, dp // 16, (dp // 2) % 8, dp % 2
    chip = dp // 2
    y = y_hi * 2 + y_lo
    turn = 1 - 2 * c
    length = len_ref[0]
    cart, seq = cart_ref.shape[1], 1024
    scale = HD ** -0.5
    factor = scale * math.log2(math.e)

    def at(dx=0, dy=0, dz=0, other=False):
        yy = lax.rem(y + dy + 8, 4)
        return (
            lax.rem(yy, 2) * 16 + lax.rem(z + dz + 16, 8) * 2 + (1 - c if other else c),
            lax.rem(x + dx + 8, 4) * 2 + yy // 2,
        )

    def peer(step):
        return lax.rem(chip + step, CHIPS)

    def ys(dy):
        yy = lax.rem(y + dy + 8, 4)
        return yy // 2, lax.rem(yy, 2)

    def xs(dx):
        return lax.rem(x + dx + 8, 4)

    slots, started = {}, []

    def send(name, ref, target, dst=None):
        assert name not in slots
        copy = pltpu.make_async_remote_copy(
            src_ref=ref, dst_ref=ref if dst is None else dst,
            send_sem=send_sem.at[len(started)], recv_sem=recv_sem.at[len(started)],
            device_id=target, device_id_type=MESH,
        )
        copy.start()
        slots[name] = copy
        started.append(copy)

    def arrived(name):
        slots[name].wait_recv()

    def main(dy, n, count=1):
        hi, lo = ys(dy)
        return wa.at[hi, lo, c, pl.ds(n, count)]

    def rest(dy, n):
        hi, lo = ys(dy)
        return wb.at[hi, lo, c, n]

    barrier = pltpu.get_barrier_semaphore()
    partners = [at(dx=1), at(dx=-1), at(dy=1), at(dy=-1), at(dy=2), at(dz=1), at(dz=-1), at(other=True)]
    peers = [(peer(step) * 2 + c, fsdp) for step in range(1, CHIPS)]
    for partner in partners + peers:
        pl.semaphore_signal(barrier, inc=1, device_id=partner, device_id_type=MESH)
    local = []
    for n, (ref, dst) in enumerate([
        (wkv_ref, kv_rows),
        (wq_ref, wa.at[y_hi, y_lo, c, 0]),
        (hidden_hbm, hidden_ref), (gain_hbm, gain_ref),
        (cos_hbm.at[:, y_hi], cos_ref), (sin_hbm.at[:, y_hi], sin_ref), (cart_hbm, cart_ref), (g_hbm, g_ref),
    ]):
        copy = pltpu.make_async_copy(ref, dst, local_sem.at[n])
        copy.start()
        local.append(copy)
    local[0].wait()
    kv_wide[...] = kv_rows[...].astype(F32)
    for i in range(2):
        wb[y_hi, y_lo, c, 0, :, i * HD:(i + 1) * HD] = kv_wide[pl.ds(i, 128, 2)].astype(BF16)
    pl.semaphore_wait(barrier, len(partners) + len(peers))

    def main_from_z(i):
        if i == 4:
            arrived(("za", 4, 1))
            arrived(("za", 4, -1))
        for way in (1, -1):
            if 0 < i < 4:
                arrived(("za", way * i))
            if i < 3:
                ref = main(0, SLOT[way * i]).at[0] if i else wq_ref
                send(("za", way * (i + 1)), ref, at(dz=-way), main(0, SLOT[way * (i + 1)]).at[0])
        if i == 3:
            for way, part in ((1, pl.ds(0, 64)), (-1, pl.ds(64, MAIN - 64))):
                send(("za", 4, way), main(0, SLOT[3 * way]).at[:, part], at(dz=-way), main(0, SLOT[4]).at[:, part])
        n, count = TICKS[i]
        for slot in range(n, n + count):
            for way in (1, -1):
                ref = main(0, slot).at[0]
                send(("ya", -way, slot), ref if i else wq_ref, at(dy=way), ref)

    def main_from_y(i):
        n, count = TICKS[i]
        for way in (1, -1):
            slot = n + (1 - way) // 2 if count == 2 else n
            arrived(("ya", way, slot))
            ref = main(way, slot)
            if count == 1:
                ref = ref.at[:, pl.ds(0, 64) if way == 1 else pl.ds(64, MAIN - 64)]
            send(("ya", 2, way, i), ref, at(dy=-way))
        if count == 2:
            arrived(("ya", 1, n + 1))
            arrived(("ya", -1, n))

    def main_to_core(i):
        n, count = TICKS[i]
        arrived(("ya", 2, 1, i))
        arrived(("ya", 2, -1, i))
        send(("ca", i), wa.at[:, :, c, pl.ds(n, count)], at(other=True))

    def rest_along_y():
        for way in (1, -1):
            send(("yb", -way), rest(0, 0), at(dy=way))

    def rest_further_along_y():
        for way in (1, -1):
            arrived(("yb", way))
            send(("yb", 2, way), rest(way, 0).at[pl.ds(0 if way == 1 else 64, 64)], at(dy=-way))

    def rest_from_z(i):
        if i == 0:
            arrived(("yb", 2, 1))
            arrived(("yb", 2, -1))
        for hi in range(2):
            if i == 4:
                arrived(("zb", 4, hi))
                continue
            for way in (1, -1):
                here = wb.at[hi, :, c, SLOT[way * i]]
                if i:
                    arrived(("zb", way * i, hi))
                if i < 3:
                    send(("zb", way * (i + 1), hi), here, at(dz=-way), wb.at[hi, :, c, SLOT[way * (i + 1)]])
                elif way == 1 - 2 * hi:
                    send(("zb", 4, hi), here, at(dz=-way), wb.at[hi, :, c, SLOT[4]])
        n, count = TICKS[i]
        send(("cb", i), wb.at[:, :, c, pl.ds(n, count)], at(other=True))

    def rows_out(part):
        n, count = X_PARTS[part]
        for way in (1, -1):
            send(("x", -way, part), xn.at[x, pl.ds(n, count)], at(dx=way))

    def rows_on(part):
        n, count = X_PARTS[part]
        for way in (1, -1):
            arrived(("x", way, part))
            send(("x", 2, way, part), xn.at[xs(way), pl.ds(n, count), (1 - way) // 2], at(dx=-way))

    def rows_ready(part):
        arrived(("x", 2, 1, part))
        arrived(("x", 2, -1, part))

    def operands(weights, n, hi):
        left = jnp.concatenate([xn[:, n, lo].reshape(512, 256) for lo in range(2)], axis=1)
        right = [weights[hi, lo, core, n] for lo in range(2) for core in range(2)]
        return left, jnp.concatenate(right, axis=0)

    def multiply_kv(n, hi):
        term = jnp.dot(*operands(wb, n, hi), preferred_element_type=F32)
        acc_kv[hi] = acc_kv[hi] + term if n else term

    def multiply_q(n, hi):
        term = jnp.dot(*operands(wa, n, hi), preferred_element_type=F32)
        acc_q[hi] = acc_q[hi] + term if n else term

    def multiply_all(i):
        arrived(("ca", i))
        arrived(("cb", i))
        n, count = TICKS[i]
        for slot in range(n, n + count):
            for hi in range(2):
                multiply_kv(slot, hi)
                multiply_q(slot, hi)

    rest_along_y()
    main_from_z(0)
    local[1].wait()
    local[2].wait()
    local[3].wait()
    hidden = hidden_ref[...].astype(F32)
    inverse = lax.rsqrt(jnp.mean(hidden * hidden, axis=-1, keepdims=True) + EPS)
    for n, step in enumerate(STEPS):
        for lo in range(2):
            k = lo * 8 + lax.rem(z + step + 8, 8)
            cols = pl.ds(pl.multiple_of(k * 256, 256), 256)
            part = hidden_ref[:, cols].astype(F32) * inverse * gain_ref[:, cols]
            xn[x, n, lo] = part.astype(BF16)
    rows_out(0)
    rows_out(1)
    for copy in local[4:]:
        copy.wait()
    vt_cart[:HD] = cart_ref[1].astype(F32).T.astype(BF16)
    vt_cart[HD:] = jnp.ones((vt_cart.shape[0] - HD, cart), BF16)
    grad[...] = jnp.zeros_like(grad)
    def grad_rows(head, j, hi):
        columns = pl.ds(pl.multiple_of(head * HD, HD), HD)
        g = g_ref[2 * j:2 * j + 2, hi, :, columns].reshape(2 * HD, HD)
        row = lax.broadcasted_iota(jnp.int32, (2 * HD, HD), 0)
        row = 4 * j * HD + (row // HD) * (2 * HD) + hi * HD + lax.rem(row, HD)
        return jnp.where(row < length, g, jnp.zeros_like(g))

    def value_products(hi):
        @pl.loop(0, 4)
        def _(head):
            for j in range(2):
                g = grad_rows(head, j, hi)
                d_keep[hi, head, j] = lax.dot_general(cart_ref[1], g, NT, preferred_element_type=F32)
                g_turned[hi, head, j] = g.astype(F32).T

    value_products(y_hi)
    rest_further_along_y()
    main_from_z(1)
    rest_from_z(0)
    main_from_y(0)
    main_from_z(2)
    rest_from_z(1)
    main_from_y(1)
    main_to_core(0)
    main_from_z(3)
    rows_on(0)
    rows_out(2)
    rest_from_z(2)
    main_from_y(2)
    main_to_core(1)
    main_from_z(4)
    value_products(1 - y_hi)
    rows_ready(0)
    multiply_all(0)
    rest_from_z(3)
    main_from_y(3)
    main_to_core(2)
    rows_on(1)
    multiply_all(1)
    main_from_y(4)
    main_to_core(3)
    rest_from_z(4)
    rows_on(2)
    rows_ready(1)
    multiply_all(2)
    theirs = 1 - y_hi

    cos, sin = cos_ref[...].reshape(512, HD), sin_ref[...].reshape(512, HD)

    def turned(part):
        return (part * cos + pltpu.roll(part, HD // 2, 1) * sin).astype(BF16).reshape(4, HD, HD)

    def finish_kv(hi, out):
        out[0] = turned(acc_kv[hi, :, :HD])
        out[1] = acc_kv[hi, :, HD:].astype(BF16).reshape(4, HD, HD)

    def spots(hi, index):
        return (index // HD) * (2 * HD) + hi * HD + lax.rem(index, HD)

    def take_keys(hi, blocks):
        spare = jnp.broadcast_to(cart_ref[0, 0:1, :], (HD, HD))
        for n in range(4):
            live = spots(hi, n * HD + lax.broadcasted_iota(jnp.int32, (HD, HD), 0)) < length
            k_new[hi, n * HD:(n + 1) * HD] = jnp.where(live, blocks[0, n], spare)
            values = jnp.where(live, blocks[1, n].astype(F32), 0.0)
            vt_new[hi, :HD, n * HD:(n + 1) * HD] = values.T.astype(BF16)
        live = spots(hi, lax.broadcasted_iota(jnp.int32, (vt_new.shape[1] - HD, 4 * HD), 1)) < length
        vt_new[hi, HD:] = jnp.where(live, 1.0, 0.0).astype(BF16)

    rows_ready(2)
    arrived(("cb", 3))
    arrived(("cb", 4))
    for n in (5, 6, 7):
        multiply_kv(n, theirs)
    first_kv = len(started)
    finish_kv(theirs, kv_out)
    send("kv", kv_out, at(dy=2), kv_in)
    main_to_core(4)
    for n in (5, 6, 7):
        multiply_kv(n, y_hi)
    finish_kv(y_hi, kv_own)
    take_keys(y_hi, kv_own)
    arrived(("ca", 3))
    for n in (5, 6):
        for hi in (0, 1):
            multiply_q(n, hi)
    arrived(("ca", 4))
    multiply_q(7, theirs)
    first_q = len(started)
    for head in range(4):
        q_out[head] = turned(acc_q[theirs, :, head * HD:(head + 1) * HD])
        if head < 3:
            send(("q", head), q_out.at[head], at(dy=2), q_in.at[head])
    for j in (1, 0):
        blocks = pl.ds(2 * j, 2)
        send(("q", 3, j), q_out.at[3, blocks], at(dy=2), q_in.at[3, blocks])
    multiply_q(7, y_hi)
    for head in range(4):
        q_own[head] = turned(acc_q[y_hi, :, head * HD:(head + 1) * HD])

    def new_scores(key_hi, hi, j, q):
        near = lax.dot_general(k_new[key_hi, 2 * j * HD:2 * (j + 1) * HD], q, NT, preferred_element_type=F32)
        key = spots(key_hi, lax.broadcasted_iota(jnp.int32, near.shape, 0))
        row = spots(hi, lax.broadcasted_iota(jnp.int32, (1, 2 * HD), 1))
        near = jnp.where(key <= row, near, -jnp.inf)
        if j == 0:
            return [near]
        return [lax.dot_general(k_new[key_hi, :2 * j * HD], q, NT, preferred_element_type=F32), near]

    def highest(tops, scores):
        for part in scores:
            tops = jnp.maximum(tops, jnp.max(part, axis=0, keepdims=True))
        return tops

    def add_values(out, key_hi, scores, top):
        first = 0
        for part in scores:
            last = first + part.shape[0]
            weights = jnp.exp2((part - top) * factor).astype(BF16)
            out += jnp.dot(vt_new[key_hi, :, first:last], weights, preferred_element_type=F32)
            first = last
        return out

    def first_part(key_hi, hi, js, qs):
        carts = [lax.dot_general(cart_ref[0], q, NT, preferred_element_type=F32) for q in qs]
        news = [new_scores(key_hi, hi, j, q) for j, q in zip(js, qs)]
        kept = []
        for scores, new in zip(carts, news):
            top = highest(jnp.max(scores, axis=0, keepdims=True), new)
            e_cart = jnp.exp2((scores - top) * factor)
            out = jnp.dot(vt_cart[...], e_cart.astype(BF16), preferred_element_type=F32)
            kept.append((e_cart, top, add_values(out, key_hi, new, top)))
        return kept

    def second_part(head, key_hi, hi, js, qs, gs, kept):
        columns = pl.ds(pl.multiple_of(head * HD, HD), HD)
        news = [new_scores(key_hi, hi, j, q) for j, q in zip(js, qs)]
        outs = []
        for new, (_, before, out) in zip(news, kept):
            top = highest(before, new)
            shrink = jnp.exp2((before - top) * factor)
            outs.append((add_values(out * shrink, key_hi, new, top), shrink))
        probs, scores = [], []
        for j, (out, shrink), (e_cart, _, _) in zip(js, outs, kept):
            inverse = 1.0 / out[HD:HD + 1]
            out = out[:HD] * inverse
            mixed_ref[2 * j:2 * j + 2, hi, :, columns] = out.T.astype(BF16).reshape(2, HD, HD)
            delta = jnp.sum(out * g_turned[hi, head, j], axis=0, keepdims=True)
            prob = e_cart * (shrink * inverse)
            scores.append((prob * (d_keep[hi, head, j] - delta)).astype(BF16))
            probs.append(prob.astype(BF16))
        join = functools.partial(jnp.concatenate, axis=0)
        grad[1] += jnp.dot(jnp.concatenate(probs, axis=1), join(gs), preferred_element_type=F32)
        grad[0] += jnp.dot(jnp.concatenate(scores, axis=1), join(qs), preferred_element_type=F32)

    def pairs(q_ref, head, hi, js=(0, 1)):
        qs = [q_ref[head, 2 * j:2 * j + 2].reshape(2 * HD, HD) for j in js]
        return qs, [grad_rows(head, j, hi) for j in js]

    both = (0, 1)

    @pl.loop(0, 4)
    def _(head):
        qs, _ = pairs(q_own, head, y_hi)
        for j, kept in enumerate(first_part(y_hi, y_hi, both, qs)):
            e_keep[head, j], top_keep[head, j], out_keep[head, j] = kept

    for copy in started[:first_kv]:
        copy.wait_send()
    arrived("kv")
    take_keys(theirs, kv_in)

    @pl.loop(0, 4)
    def _(head):
        kept = [(e_keep[head, j], top_keep[head, j], out_keep[head, j]) for j in both]
        second_part(head, theirs, y_hi, both, *pairs(q_own, head, y_hi), kept)

    @pl.loop(0, 3)
    def _(head):
        pltpu.make_async_remote_copy(
            src_ref=q_out.at[head], dst_ref=q_in.at[head], send_sem=send_sem.at[first_q + head],
            recv_sem=recv_sem.at[first_q + head], device_id=at(dy=2), device_id_type=MESH,
        ).wait_recv()
        qs, gs = pairs(q_in, head, theirs)
        second_part(head, theirs, theirs, both, qs, gs, first_part(y_hi, theirs, both, qs))

    for j in (1, 0):
        arrived(("q", 3, j))
        qs, gs = pairs(q_in, 3, theirs, (j,))
        second_part(3, theirs, theirs, (j,), qs, gs, first_part(y_hi, theirs, (j,), qs))

    rows = cart
    send("core_sum", grad.at[1 - c], at(other=True), from_core)
    arrived("core_sum")
    half[...] = (grad[c] + from_core[...]).reshape(half.shape)
    to_chips[...] = half[...].astype(BF16)
    for step in FAR_FIRST:
        send(("rs", step), to_chips.at[peer(step)], peers[step - 1], from_chips.at[step])
    done = len(started)
    for copy in started[first_kv:]:
        copy.wait_send()
    total = half[chip]
    for step in reversed(FAR_FIRST):
        arrived(("rs", step))
        total += from_chips[step].astype(F32)
    total = total * jnp.where(c == 0, scale, 1.0)
    gathered[chip] = total.astype(BF16)
    for step in FAR_FIRST:
        send(("ag", step), gathered.at[chip], peers[step - 1])
    for step in range(1, CHIPS):
        arrived(("ag", step))
    send("core_back", gathered, at(other=True), other)
    sum_ref[c] = gathered[...].reshape(rows, HD)
    arrived("core_back")
    sum_ref[1 - c] = other[...].reshape(rows, HD)
    for copy in started[done:]:
        copy.wait_send()


def rope_tables(cart, seq):
    frequency = np.power(np.float32(ROPE_BASE), np.arange(HD // 2, dtype=np.float32) * np.float32(-2.0 / HD))
    angles = (cart + np.arange(seq, dtype=np.float32))[:, None] * frequency.astype(np.float32)[None, :]
    cos, sin = np.cos(angles), np.sin(angles)
    shape = (seq // 256, 2, 128, HD)
    return (
        np.concatenate([cos, cos], axis=1).astype(np.float32).reshape(shape),
        np.concatenate([-sin, sin], axis=1).astype(np.float32).reshape(shape),
    )


def tail_kernel(mixed_ref, sum_ref, mixed_out, sum_out):
    mixed_out[...] = mixed_ref[...]
    sum_out[...] = sum_ref[...].astype(F32)


def on_device(hidden_in, lengths, cartridge, norm_gain, w_query, w_keyval, cotangent):
    cart = cartridge.shape[1]
    vmem, hbm = pl.BlockSpec(memory_space=pltpu.VMEM), pl.BlockSpec(memory_space=pltpu.HBM)
    cos, sin = rope_tables(cart, 1024)
    copies, share = 120, cart // CHIPS
    mixed, summed = pl.pallas_call(
        layer_kernel,
        name="layer",
        out_shape=(
            jax.ShapeDtypeStruct((4, 2, 128, 512), BF16),
            jax.ShapeDtypeStruct((2, cart, HD), BF16),
        ),
        in_specs=[pl.BlockSpec(memory_space=pltpu.SMEM)] + [hbm] * 8,
        out_specs=(vmem,) * 2,
        scratch_shapes=[
            pltpu.VMEM((128, 4096), BF16),
            pltpu.VMEM((1, 4096), F32),
            pltpu.VMEM((4, 128, HD), F32),
            pltpu.VMEM((4, 128, HD), F32),
            pltpu.VMEM((2, cart, HD), BF16),
            pltpu.VMEM((4, 2, 128, 512), BF16),
            pltpu.VMEM((4, 8, 2, 128, 256), BF16),
            pltpu.VMEM((2, 2, 2, 8, MAIN, 512), BF16),
            pltpu.VMEM((2, 2, 2, 8, 128, 256), BF16),
            pltpu.VMEM((2, 512, 512), F32),
            pltpu.VMEM((2, 512, 256), F32),
            pltpu.VMEM((4, 4, 128, HD), BF16),
            pltpu.VMEM((2, 4, 128, HD), BF16),
            pltpu.VMEM((4, 4, 128, HD), BF16),
            pltpu.VMEM((2, 4, 128, HD), BF16),
            pltpu.VMEM((4, 4, 128, HD), BF16),
            pltpu.VMEM((2, 4, 128, HD), BF16),
            pltpu.VMEM((2, 512, HD), BF16),
            pltpu.VMEM((HD + 16, cart), BF16),
            pltpu.VMEM((2, HD + 16, 512), BF16),
            pltpu.VMEM((4, 2, cart, 256), F32),
            pltpu.VMEM((2, 4, 2, cart, 256), F32),
            pltpu.VMEM((2, 4, 2, HD, 256), F32),
            pltpu.VMEM((4, 2, 1, 256), F32),
            pltpu.VMEM((4, 2, HD + 16, 256), F32),
            pltpu.VMEM((2, cart, HD), F32),
            pltpu.VMEM((cart, HD), F32),
            pltpu.VMEM((CHIPS, share, HD), F32),
            pltpu.VMEM((CHIPS, share, HD), BF16),
            pltpu.VMEM((CHIPS, share, HD), BF16),
            pltpu.VMEM((CHIPS, share, HD), BF16),
            pltpu.VMEM((CHIPS, share, HD), BF16),
            pltpu.VMEM((256, HD), BF16),
            pltpu.VMEM((256, HD), F32),
            pltpu.SemaphoreType.DMA((8,)),
            pltpu.SemaphoreType.DMA((copies,)),
            pltpu.SemaphoreType.DMA((copies,)),
        ],
        compiler_params=pltpu.CompilerParams(collective_id=0, has_side_effects=True, vmem_limit_bytes=60 << 20),
    )(lengths, hidden_in, norm_gain.reshape(1, -1), w_query, w_keyval.reshape(256, HD), cos, sin, cartridge,
      cotangent.reshape(4, 2, 128, 512))
    blocks = (
        pl.BlockSpec((1, 2, 128, 512), lambda i: (i, 0, 0, 0)),
        pl.BlockSpec((1, cart // 2, HD), lambda i: (i // 2, i % 2, 0)),
    )
    mixed, summed = pl.pallas_call(
        tail_kernel,
        name="tail",
        out_shape=(
            jax.ShapeDtypeStruct(mixed.shape, BF16),
            jax.ShapeDtypeStruct(summed.shape, F32),
        ),
        grid=(4,),
        in_specs=blocks,
        out_specs=blocks,
    )(mixed, summed)
    return mixed.reshape(1024, 512), summed


def solution(mesh):
    in_specs = (
        P(("dp", "fsdp"), None),
        P("dp"),
        P(None, None, "fsdp"),
        P(),
        P("dp", "fsdp"),
        P("dp", None, "fsdp"),
        P("dp", "fsdp"),
    )
    out_specs = (P("dp", "fsdp"), P(None, None, "fsdp"))
    return jax.shard_map(on_device, mesh=mesh, in_specs=in_specs, out_specs=out_specs, check_vma=False)
```
